256 devices in a mesh: gx: 8 (over z), gy: 32 (over y, x, core).
Axes of the slice: x: 4, y: 4, z: 8, core: 2. Of those that a mesh axis runs over, the one named last changes fastest.
Arguments:
- reference_scan: bfloat16 [256, 1024, 128], P('gx', 'gy'), may hold values from -6 to 6
- deformed_scan: bfloat16 [256, 1024, 128], P('gx', 'gy'), may hold values from -6 to 6
- source_column: int32 [8, 32, 64, 1], P('gx'), may hold values from 0 to 31, as said below
Outputs:
- update: float32 [3, 16, 64, 9], P(None, 'gx', 'gy')
- cg_residual: float32 [3, 16, 64, 9], P(None, 'gx', 'gy')
The draws below stay inside these ranges and needn't reach their ends.
Inputs may be any that keep to these rules, and one draw needn't show every extreme that they name: source_column[p, q, b, 0] is q - 1, q or q + 1. Within one brick's 64 blocks at most 16 come from column q - 1 and at most 16 from column q + 1; in every draw some brick takes exactly 16 blocks from column q - 1 and some brick exactly 16 from column q + 1.
All inputs are finite; a program needn't handle non-finite values.
Results may differ from the reference program's by a relative error of at most 0.0003.
Values may be sent and summed in bfloat16 or wider, within the bound.
A program may use at most 64 MiB of HBM per device.

```python
import jax
import jax.numpy as jnp
from jax import lax

BX = 32
BY = 32
BZ = 128
E = 16
ITERS = 4
NBLK = 64
CAP = 16
NX = 256
NY = 1024
NZN = 9
GNX = 16
GNY = 64
N_GX = 8
N_GY = 32


def draw_source_column(key, part):
    keys = jax.random.split(jax.random.fold_in(key, 17), 7)
    left_count = jax.random.randint(keys[0], (N_GX, N_GY), 0, CAP + 1)
    right_count = jax.random.randint(keys[1], (N_GX, N_GY), 0, CAP + 1)
    rows = jnp.arange(N_GX, dtype=jnp.int32)[:, None]
    cols = jnp.arange(N_GY, dtype=jnp.int32)[None, :]
    left_row = jax.random.randint(keys[2], (), 0, N_GX)
    left_col = jax.random.randint(keys[3], (), 1, N_GY)
    right_row = jax.random.randint(keys[4], (), 0, N_GX)
    right_col = jax.random.randint(keys[5], (), 0, N_GY - 1)
    left_count = jnp.where((rows == left_row) & (cols == left_col), CAP, left_count)
    right_count = jnp.where((rows == right_row) & (cols == right_col), CAP, right_count)
    scores = jax.random.randint(keys[6], (N_GX, N_GY, NBLK), 0, 1 << 20)
    scores = scores * NBLK + jnp.arange(NBLK, dtype=jnp.int32)[None, None, :]
    order = jnp.argsort(scores, axis=2)
    rank = jnp.argsort(order, axis=2).astype(jnp.int32)
    offset = jnp.where(rank < left_count[:, :, None], -1, jnp.where(rank < (left_count + right_count)[:, :, None], 1, 0))
    column = jnp.clip(cols[:, :, None] + offset, 0, N_GY - 1).astype(jnp.int32)
    return column[:, :, :, None]


def shard_levels(key, shape, cuts, low, top_value):
    def one(dim, blocks):
        steps = jax.random.uniform(jax.random.fold_in(jax.random.fold_in(key, 6), dim), (blocks,), jnp.float32, low / len(cuts), top_value / len(cuts))
        return jnp.repeat(jnp.exp(steps), shape[dim] // blocks).reshape((-1,) + (1,) * (len(shape) - dim - 1))

    factor_of = one(*cuts[0])
    for cut in cuts[1:]:
        factor_of = factor_of * one(*cut)
    return factor_of


def noise(own_key, dims, scale, most, cuts=(), kind=jnp.bfloat16):
    values = jax.random.normal(own_key, dims, jnp.float32) * scale
    if len(cuts) > 0:
        values = shard_levels(own_key, dims, cuts, -0.22, 0.18) * values
    return jnp.clip(values, min=-most, max=most).astype(kind)


def setup_inputs(seed: int = 0) -> dict:
    splits = jax.random.split(jax.random.key(seed), 4)
    return {
        "reference_scan": noise(splits[0], (NX, NY, BZ), 1.0, 6.0, ((0, 8), (1, 32))),
        "deformed_scan": noise(splits[1], (NX, NY, BZ), 1.0, 6.0, ((0, 8), (1, 32))),
        "source_column": draw_source_column(jax.random.fold_in(splits[3], 71), 0),
    }


damping = 0.1


def shape_matrix(count, nodes, edge):
    position = jnp.arange(count, dtype=jnp.float32)[:, None]
    anchor = jnp.arange(nodes, dtype=jnp.float32)[None, :] * edge
    return jnp.maximum(0.0, 1.0 - jnp.abs(position - anchor) / edge)


def reference(reference_scan, deformed_scan, source_column):
    blocks = deformed_scan.reshape(N_GX, BX // 8, 8, N_GY, BY // 8, 8, 4, BZ // 4)
    blocks = blocks.transpose(0, 3, 1, 4, 6, 2, 5, 7).reshape(N_GX, N_GY, NBLK, 16 * BZ)
    row_index = jnp.arange(N_GX, dtype=jnp.int32)[:, None, None]
    block_index = jnp.arange(NBLK, dtype=jnp.int32)[None, None, :]
    chosen = blocks[row_index, source_column[:, :, :, 0].astype(jnp.int32), block_index]
    warped = chosen.reshape(N_GX, N_GY, BX // 8, BY // 8, 4, 8, 8, BZ // 4)
    warped = warped.transpose(0, 2, 5, 1, 3, 6, 4, 7).reshape(NX, NY, BZ)
    field = reference_scan.astype(jnp.float32)
    padded = jnp.pad(field, 1)
    scale = 1.0 / (2.0 * E)
    gradient = [
        (padded[2:, 1:-1, 1:-1] - padded[:-2, 1:-1, 1:-1]) * scale,
        (padded[1:-1, 2:, 1:-1] - padded[1:-1, :-2, 1:-1]) * scale,
        (padded[1:-1, 1:-1, 2:] - padded[1:-1, 1:-1, :-2]) * scale,
    ]
    misfit = field - warped.astype(jnp.float32)
    matrix_x = shape_matrix(NX, GNX, float(E))
    matrix_y = shape_matrix(NY, GNY, float(E))
    matrix_z = shape_matrix(BZ, NZN, float(E))
    highest = lax.Precision.HIGHEST

    def spread(nodal):
        temp = jnp.einsum("ijk,zk->ijz", nodal, matrix_z, precision=highest)
        temp = jnp.einsum("ijz,yj->iyz", temp, matrix_y, precision=highest)
        return jnp.einsum("iyz,xi->xyz", temp, matrix_x, precision=highest)

    def collect(voxels):
        temp = jnp.einsum("xyz,xi->iyz", voxels, matrix_x, precision=highest)
        temp = jnp.einsum("iyz,yj->ijz", temp, matrix_y, precision=highest)
        return jnp.einsum("ijz,zk->ijk", temp, matrix_z, precision=highest)

    def operate(nodal):
        along = gradient[0] * spread(nodal[0])
        along = along + gradient[1] * spread(nodal[1])
        along = along + gradient[2] * spread(nodal[2])
        back = jnp.stack([collect(gradient[c] * along) for c in range(3)])
        return back + damping * nodal

    rhs = jnp.stack([collect(gradient[c] * misfit) for c in range(3)])
    update = jnp.zeros_like(rhs)
    residual = rhs
    direction = rhs
    norm_now = jnp.sum(residual * residual)
    for turn in range(ITERS):
        image = operate(direction)
        alpha = norm_now / jnp.sum(direction * image)
        update = update + alpha * direction
        residual = residual - alpha * image
        norm_next = jnp.sum(residual * residual)
        direction = residual + (norm_next / norm_now) * direction
        norm_now = norm_next
    return update, residual
```

```python
import functools

import jax
import jax.numpy as jnp
import ml_dtypes
import numpy as np
from jax import lax
from jax.experimental import pallas as pl
from jax.experimental.pallas import tpu as pltpu
from jax.sharding import PartitionSpec as P

MESH = pl.DeviceIdType.MESH
E = 16
ITERS = 4
DAMPING = 0.1
NGX, NGY = 8, 32
F32, BF16 = jnp.float32, jnp.bfloat16

NEIGHBOURS = [(dx, dy) for dx in (-1, 0, 1) for dy in (-1, 0, 1) if (dx, dy) != (0, 0)]
SOURCES = [(bx, by) for bx in (-2, -1, 0, 1) for by in (-2, -1, 0, 1) if (bx, by) != (0, 0)]
PAIRS = [(0, 0), (1, 1), (2, 2), (0, 1), (1, 2), (2, 0)]


def hat(position):
    return np.maximum(0.0, 1.0 - np.abs(position) / E)


def chain(count, nodes):
    position = np.arange(count)
    w = np.stack([hat(position - E * n) for n in range(nodes)])
    out = []
    for n in range(nodes):
        out.append(w[n] * w[n])
        if n + 1 < nodes:
            out.append(w[n] * w[n + 1])
    return w, np.stack(out)


def constants():
    wy, cy = chain(32, 3)
    wz, cz = chain(128, 9)
    scale = 1.0 / 1024.0
    ymat = np.zeros((48, 192))
    for m in range(5):
        for p in range(6):
            ymat[m * 8 + p, p * 32 : (p + 1) * 32] = cy[m] * scale
    zd, zf = np.zeros((128, 16)), np.zeros((128, 16))
    zd[:, :9] = cz[0::2].T
    zf[:, :8] = cz[1::2].T
    wmat = np.zeros((5, 128, 4, 8, 16))
    D0, F0, D1, F1, D2 = range(5)
    place = {
        (0, 0): (F0, zd), (0, 1): (F1, zd), (0, 2): (D1, zd), (0, 3): (D2, zd),
        (0, 4): (F0, zf), (0, 5): (F1, zf), (0, 6): (D1, zf), (0, 7): (D2, zf),
        (1, 2): (D0, zd), (1, 3): (D1, zd), (1, 4): (D2, zd), (1, 5): (F0, zd), (1, 6): (F1, zd),
        (2, 2): (D0, zf), (2, 3): (D1, zf), (2, 4): (D2, zf), (2, 5): (F0, zf), (2, 6): (F1, zf),
        (3, 4): (D0, zd), (3, 5): (F0, zd), (3, 6): (D0, zf), (3, 7): (F0, zf),
    }
    for (group, block), (m, z) in place.items():
        wmat[m, :, group, block, :] = z
    wmat = wmat.reshape(640, 512)
    yr = np.zeros((32, 96))
    for n in range(3):
        for r in range(8):
            c = r % 3
            yr[n * 8 + r, c * 32 : (c + 1) * 32] = wy[n] / 32.0
    wr = np.zeros((3, 128, 8, 16))
    for n in range(3):
        wr[n, :, 2 + n, :9] = wz.T
    wr = wr.reshape(384, 128)
    dz = np.zeros((128, 128))
    for z in range(128):
        if z + 1 < 128:
            dz[z + 1, z] = 1.0
        if z > 0:
            dz[z - 1, z] = -1.0
    lanes = np.arange(128)
    spread = (np.arange(64)[:, None] % 4 == lanes[None, :] // 32).astype(np.float64)
    small = np.zeros((256, 256))
    cast = lambda a: a.astype(ml_dtypes.bfloat16)
    return [cast(a) for a in (ymat, wmat, yr, wr, dz, spread)]


def pieces(x):
    hi = x.astype(BF16)
    rest = x - hi.astype(F32)
    mid = rest.astype(BF16)
    low = (rest - mid.astype(F32)).astype(BF16)
    return hi, mid, low


def mm(a, b):
    return jnp.dot(a, b, preferred_element_type=F32)


def kernel(
    ref_h, def_h, table, ymat, wmat_h, yr, wr, dz, spread,
    upd_out, res_out,
    ref_v, own_v, lo_v, hi_v, fs, gs, mask_s, yface, xlo, xhi, ylo, yhi,
    xs, t2, ksend, krecv, rx, rt2, rsend, rrecv, kf, wmat, vsend, vrecv,
    asrc, a1, b1src, b1, asrc2, a2, b2src, b2,
    lsem, fsend, frecv, ksem_s, ksem_r, rsem_s, rsem_r, vsem_s, vsem_r, arsem_s, arsem_r,
):
    gx, gy = lax.axis_index("gx"), lax.axis_index("gy")

    def at(dx, dy):
        return (lax.rem(gx + (dx + NGX), NGX), lax.rem(gy + (dy + NGY), NGY))

    barrier = pltpu.get_barrier_semaphore()
    partners = [at(0, m) for m in range(1, NGY)] + [at(m, 0) for m in range(1, NGX)]
    partners += [at(bx, by) for bx, by in SOURCES if bx != 0 and by != 0]
    for partner in partners:
        pl.semaphore_signal(barrier, inc=1, device_id=partner, device_id_type=MESH)

    load_ref = pltpu.make_async_copy(ref_h, ref_v, lsem.at[0])
    load_own = pltpu.make_async_copy(def_h, own_v, lsem.at[1])
    load_w = pltpu.make_async_copy(wmat_h, wmat, lsem.at[2])
    load_ref.start()
    load_own.start()
    load_w.start()

    def flag(condition):
        return jnp.where(condition, 1.0, 0.0).astype(F32)

    xlo_ok, xhi_ok = flag(gx > 0), flag(gx < NGX - 1)
    ylo_ok, yhi_ok = flag(gy > 0), flag(gy < NGY - 1)

    row = (table[gy] - gy).astype(F32)
    r16 = lax.broadcasted_iota(jnp.int32, (16, 64), 0)
    c64 = lax.broadcasted_iota(jnp.int32, (16, 64), 1)
    picked = jnp.where(c64 // 4 == r16, jnp.broadcast_to(row, (16, 64)), 0.0).astype(BF16)
    mask_s[...] = mm(picked, spread[...])

    load_ref.wait()
    for x in range(32):
        plane = ref_v[x]
        fs[x + 1, 8:40, :] = plane.astype(F32)
        gs[2, x] = mm(plane, dz[...])
    yface[0] = jnp.concatenate([fs[x + 1, 39:40, :] for x in range(32)], axis=0).astype(BF16)
    yface[1] = jnp.concatenate([fs[x + 1, 8:9, :] for x in range(32)], axis=0).astype(BF16)

    pl.semaphore_wait(barrier, len(partners))

    def send(src, dst, s, r, to):
        copy = pltpu.make_async_remote_copy(
            src_ref=src, dst_ref=dst, send_sem=s, recv_sem=r, device_id=to, device_id_type=MESH
        )
        copy.start()
        return copy

    c_ylo = send(yface.at[0], ylo, fsend.at[0], frecv.at[0], at(0, 1))
    c_yhi = send(yface.at[1], yhi, fsend.at[1], frecv.at[1], at(0, -1))
    c_xlo = send(ref_v.at[31], xlo, fsend.at[2], frecv.at[2], at(1, 0))
    c_xhi = send(ref_v.at[0], xhi, fsend.at[3], frecv.at[3], at(-1, 0))
    load_own.wait()
    c_dlo = send(own_v, lo_v, fsend.at[4], frecv.at[4], at(0, 1))
    c_dhi = send(own_v, hi_v, fsend.at[5], frecv.at[5], at(0, -1))
    c_xlo.wait_recv()
    c_xhi.wait_recv()
    c_ylo.wait_recv()
    c_yhi.wait_recv()
    fs[0, 8:40, :] = xlo[...].astype(F32) * xlo_ok
    fs[33, 8:40, :] = xhi[...].astype(F32) * xhi_ok
    face_lo = ylo[...].astype(F32) * ylo_ok
    face_hi = yhi[...].astype(F32) * yhi_ok
    for x in range(32):
        fs[x + 1, 7:8, :] = face_lo[x : x + 1]
        fs[x + 1, 40:41, :] = face_hi[x : x + 1]

    for ey in range(2):
        r = 8 + 16 * ey
        y = slice(16 * ey, 16 * ey + 16)
        moments = []
        for ex in range(2):
            def step(t, carry, ex=ex, r=r, y=y):
                x = 16 * ex + t
                g = (
                    fs[x + 2, r : r + 16, :] - fs[x, r : r + 16, :],
                    fs[x + 1, r + 1 : r + 17, :] - fs[x + 1, r - 1 : r + 15, :],
                    gs[2, x, y, :],
                )
                gs[0, x, y, :] = g[0]
                gs[1, x, y, :] = g[1]
                out = []
                for p, (c, d) in enumerate(PAIRS):
                    s1, s2, s3 = carry[p]
                    s1 = s1 + g[c] * g[d]
                    s2 = s2 + s1
                    s3 = s3 + s2
                    out.append((s1, s2, s3))
                return tuple(out)

            zero = jnp.zeros((16, 128), F32)
            sums = lax.fori_loop(0, 16, step, tuple((zero,) * 3 for _ in PAIRS), unroll=4)
            weighted = []
            for s1, s2, s3 in sums:
                m00 = (2.0 * s3 - s2) * (1.0 / 256.0)
                first = s2 * (1.0 / 16.0)
                weighted.append((m00, first - m00, s1 - 2.0 * first + m00))
            moments.append(weighted)
        for p in range(6):
            (a00, a01, a11), (b00, b01, b11) = moments[0][p], moments[1][p]
            rows = slice(p * 32 + 16 * ey, p * 32 + 16 * ey + 16)
            for u, value in enumerate((a00, a01, a11 + b00, b01, b11)):
                xs[u, rows, :] = value

    t2[40:48, :] = jnp.zeros((8, 640), F32)
    for u in range(5):
        hi, mid, low = pieces(xs[u])
        t = mm(ymat[...], hi) + mm(ymat[...], mid) + mm(ymat[...], low)
        for m in range(5):
            t2[8 * u : 8 * u + 8, 128 * m : 128 * m + 128] = t[8 * m : 8 * m + 8]
    load_w.wait()
    stacked = jnp.concatenate(pieces(t2[...]), axis=0)
    done = mm(stacked, wmat[...])
    done = done[:48] + done[48:96] + done[96:144]
    for u in range(5):
        for group in range(4):
            ksend[group, u] = done[8 * u : 8 * u + 8, 128 * group : 128 * group + 128]

    GROUP = {1: (0, 1), 0: (1, 2), -1: (3, 1)}
    UNIT = {1: (1, 4), 0: (0, 5), -1: (0, 2)}
    kcopies = []
    for n, (dx, dy) in enumerate(NEIGHBOURS):
        g0, gn = GROUP[dy]
        u0, un = UNIT[dx]
        kcopies.append(
            send(
                ksend.at[pl.ds(g0, gn), pl.ds(u0, un)],
                krecv.at[1 - dx, pl.ds(g0, gn), pl.ds(u0, un)],
                ksem_s.at[n], ksem_r.at[n], at(dx, dy),
            )
        )
    krecv[1, 1:3] = ksend[1:3]

    c_dlo.wait_recv()
    c_dhi.wait_recv()
    for ey in range(2):
        r = 8 + 16 * ey
        y = slice(16 * ey, 16 * ey + 16)
        parts = []
        for ex in range(2):
            carry = tuple((jnp.zeros((16, 128), F32),) * 2 for _ in range(3))
            for xb in range(2):
                k = (2 * ex + xb) * 4 + 2 * ey
                off = jnp.concatenate(
                    [jnp.broadcast_to(mask_s[k + h : k + h + 1, :], (8, 128)) for h in range(2)], axis=0
                )
                below, above = off < -0.5, off > 0.5

                def step(t, carry, below=below, above=above, ex=ex, xb=xb, r=r, y=y):
                    x = 16 * ex + 8 * xb + t
                    warped = jnp.where(
                        below, lo_v[x, y, :].astype(F32),
                        jnp.where(above, hi_v[x, y, :].astype(F32), own_v[x, y, :].astype(F32)),
                    )
                    misfit = fs[x + 1, r : r + 16, :] - warped
                    out = []
                    for c in range(3):
                        s1, s2 = carry[c]
                        s1 = s1 + gs[c, x, y, :] * misfit
                        out.append((s1, s2 + s1))
                    return tuple(out)

                carry = lax.fori_loop(0, 8, step, carry, unroll=4)
            parts.append([(s2 * (1.0 / 16.0), s1 - s2 * (1.0 / 16.0)) for s1, s2 in carry])
        for c in range(3):
            (a0, a1_), (b0, b1_) = parts[0][c], parts[1][c]
            rows = slice(c * 32 + 16 * ey, c * 32 + 16 * ey + 16)
            for n, value in enumerate((a0, a1_ + b0, b1_)):
                rx[n, rows, :] = value
    rt2[24:32, :] = jnp.zeros((8, 384), F32)
    for n in range(3):
        hi, mid, low = pieces(rx[n])
        t = mm(yr[...], hi) + mm(yr[...], mid) + mm(yr[...], low)
        for m in range(3):
            rt2[8 * n : 8 * n + 8, 128 * m : 128 * m + 128] = t[8 * m : 8 * m + 8]
    stacked = jnp.concatenate(pieces(rt2[...]), axis=0)
    done = mm(stacked, wr[...])
    done = done[:32] + done[32:64] + done[64:96]
    for n in range(3):
        rsend[n] = done[8 * n : 8 * n + 8]
    rcopies = []
    for n, (bx, by) in enumerate(SOURCES):
        rcopies.append(
            send(rsend, rrecv.at[bx + 2, by + 2], rsem_s.at[n], rsem_r.at[n], at(-bx, -by))
        )
    rrecv[2, 2] = rsend[...]

    lane = lax.broadcasted_iota(jnp.int32, (8, 128), 1)
    sub = lax.broadcasted_iota(jnp.int32, (8, 128), 0)
    slot, depth = lane // 16, lane % 16

    def roll(x, shift):
        shift = shift % 128
        return x if shift == 0 else pltpu.roll(x, shift, 1)

    for copy in kcopies:
        copy.wait_recv()
    in_a_diag = jnp.where(slot == 1, 1.0, jnp.where(slot == 2, ylo_ok, 0.0))
    in_b_diag = (slot >= 2) & (slot <= 4)
    for e in range(9):
        def entry(group, e=e):
            if e == 3:
                return krecv[0, group, 4] * xlo_ok + krecv[1, group, 0]
            if e == 7:
                return krecv[1, group, 4] + krecv[2, group, 0]
            if e < 3:
                return krecv[0, group, e + 1]
            if e < 7:
                return krecv[1, group, e - 3]
            return krecv[2, group, 1]

        a, b0, b1_, c = [entry(group) for group in range(4)]

        def diag(a, b, c):
            return a * in_a_diag + jnp.where(in_b_diag, b, 0.0) + jnp.where(slot == 4, c, 0.0)

        def off_diag(a, b, c):
            return jnp.where(slot < 2, a, jnp.where(slot < 4, b, jnp.where(slot == 4, c, 0.0)))

        dd = diag(roll(a, -16), b0, c)
        fd = off_diag(a, roll(b0, -48), roll(c, -16))
        df = diag(roll(a, -80), b1_, roll(c, -32))
        ff = off_diag(roll(a, -64), roll(b1_, -48), roll(c, -48))
        kf[e, 4] = dd
        kf[e, 5] = df
        kf[e, 3] = roll(df, 1)
        kf[e, 7] = fd
        kf[e, 1] = roll(fd, 16)
        kf[e, 8] = ff
        kf[e, 6] = roll(ff, 1)
        kf[e, 2] = roll(ff, 16)
        kf[e, 0] = roll(ff, 17)

    lane_j = 2 * gy + slot - 2
    lane_ok = (lane_j >= 0) & (lane_j < 64) & (slot < 6) & (depth < 9)
    lane_mask = jnp.where(lane_ok, 1.0, 0.0)
    node_mask = {i: lane_mask * flag((2 * gx + i >= 0) & (2 * gx + i < 16)) for i in range(-2, 4)}
    own_mask = jnp.where((slot >= 2) & (slot < 4) & (depth < 9), 1.0, 0.0)

    def apply(v, rows):
        need = sorted({i + ox for i in rows for ox in (-1, 0, 1)})
        first, second = {}, {}
        for i in need:
            second[i] = v[i]
            first[i] = jnp.where(sub < 3, v[i], pltpu.roll(v[i], 7, 0))
        acc1 = {i: jnp.zeros((8, 128), F32) for i in rows}
        acc2 = {i: jnp.zeros((8, 128), F32) for i in rows}
        for o in range(9):
            oy, oz = o // 3 - 1, o % 3 - 1
            s1 = {i: roll(first[i], -(16 * oy + oz)) for i in need}
            s2 = {i: roll(second[i], -(16 * oy + oz)) for i in need}
            for i in rows:
                for ox in (-1, 0, 1):
                    k = kf[2 * i + 3 + ox, o]
                    acc1[i] = acc1[i] + k * s1[i + ox]
                    acc2[i] = acc2[i] + k * s2[i + ox]
        out = {}
        for i in rows:
            total = acc1[i] + pltpu.roll(acc1[i], 5, 0)
            total = total + jnp.where(sub == 0, pltpu.roll(acc2[i], 3, 0), pltpu.roll(acc2[i], 6, 0))
            out[i] = jnp.where(sub < 3, total, jnp.where(sub < 6, pltpu.roll(total, 3, 0), pltpu.roll(total, 6, 0)))
        return out

    for copy in rcopies:
        copy.wait_recv()
    w0 = {}
    lo2_x, lo2_y = flag(gx > 1), flag(gy > 1)
    x_ok = {-2: lo2_x, -1: xlo_ok, 0: None, 1: None}
    y_ok = {-2: lo2_y, -1: ylo_ok, 0: None, 1: None}
    for i in range(-2, 4):
        total = None
        for by in (-2, -1, 0, 1):
            part = None
            for bx in (-2, -1, 0, 1):
                n = i - 2 * bx
                if 0 <= n <= 2:
                    term = rrecv[bx + 2, by + 2, n]
                    if x_ok[bx] is not None:
                        term = term * x_ok[bx]
                    part = term if part is None else part + term
            part = roll(part, 32 * by)
            if y_ok[by] is not None:
                part = part * y_ok[by]
            total = part if total is None else total + part
        w0[i] = total * node_mask[i]

    w1 = apply(w0, (-1, 0, 1, 2))
    w1 = {i: w1[i] * node_mask[i] for i in w1}
    w2_own = apply(w1, (0, 1))
    for i in range(2):
        vsend[i] = w2_own[i] * own_mask
    vcopies = []
    for n, (dx, dy) in enumerate(NEIGHBOURS):
        vcopies.append(
            send(vsend, vrecv.at[1 - dx, 1 - dy], vsem_s.at[n], vsem_r.at[n], at(dx, dy))
        )
    vrecv[1, 1] = vsend[...]

    counted = jnp.where(sub < 3, own_mask, 0.0)

    def dots(rows_of_pairs, count):
        out = []
        for a, b in rows_of_pairs:
            product = (a[0] * b[0] + a[1] * b[1]) * counted
            out.append(jnp.sum(product, axis=0, keepdims=True))
        out += [jnp.zeros((1, 128), F32)] * (count - len(out))
        return jnp.concatenate(out, axis=0)

    def all_sum(value, which, src_a, slots_a, src_b, slots_b):
        src_a[...] = value
        slots_a[gy] = value
        copies = []
        for m in range(1, NGY):
            copies.append(send(src_a, slots_a.at[gy], arsem_s.at[which, 0], arsem_r.at[which, 0], at(0, m)))
        def finish():
            pltpu.make_async_copy(slots_a.at[pl.ds(0, NGY - 1)], slots_a.at[pl.ds(0, NGY - 1)], arsem_r.at[which, 0]).wait()
            part = jnp.sum(slots_a[...], axis=0)
            src_b[...] = part
            slots_b[gx] = part
            for m in range(1, NGX):
                send(src_b, slots_b.at[gx], arsem_s.at[which, 1], arsem_r.at[which, 1], at(m, 0))
            pltpu.make_async_copy(slots_b.at[pl.ds(0, NGX - 1)], slots_b.at[pl.ds(0, NGX - 1)], arsem_r.at[which, 1]).wait()
            return jnp.sum(jnp.sum(slots_b[...], axis=0), axis=1, keepdims=True)
        return finish

    finish = all_sum(dots([(w0, w0), (w0, w1), (w1, w1)], 8), 0, asrc, a1, b1src, b1)

    for copy in vcopies:
        copy.wait_recv()
    w2 = {}
    for i in range(-2, 4):
        bx, n = i // 2, i % 2
        total = vrecv[bx + 1, 1, n] + roll(vrecv[bx + 1, 0, n], -32) + roll(vrecv[bx + 1, 2, n], 32)
        w2[i] = total * node_mask[i]
    w3 = apply(w2, (-1, 0, 1, 2))
    w3 = {i: w3[i] * node_mask[i] for i in w3}

    sums = finish()
    m0, m1, m2 = sums[0:1], sums[1:2], sums[2:3]
    mu = m1 / m0
    var = jnp.maximum(m2 / m0 - mu * mu, 1e-6 * mu * mu)
    sigma = jnp.sqrt(var)
    inv = 1.0 / sigma
    rows = (-1, 0, 1, 2)
    q0 = {i: w0[i] for i in rows}
    q1 = {i: (w1[i] - mu * w0[i]) * inv for i in rows}
    kq1 = {i: (w2[i] - mu * w1[i]) * inv for i in rows}
    kkq1 = {i: (w3[i] - mu * w2[i]) * inv for i in rows}
    q2 = {i: (kq1[i] - mu * q1[i]) * inv - q0[i] for i in rows}
    kq2 = {i: (kkq1[i] - mu * kq1[i]) * inv - w1[i] for i in rows}
    q3 = {i: (kq2[i] - mu * q2[i]) * inv - q1[i] for i in rows}
    kq3 = apply(q3, (0, 1))
    q4 = {i: (kq3[i] - mu * q3[i]) * inv - q2[i] for i in (0, 1)}
    basis = [q0, q1, q2, q3, q4]
    pairs = [(i, j) for i in range(5) for j in range(i, 5) if (i, j) != (4, 4)]
    gram = all_sum(dots([(basis[i], basis[j]) for i, j in pairs], 16), 1, asrc2, a2, b2src, b2)()
    G = {}
    for n, (i, j) in enumerate(pairs):
        G[i, j] = G[j, i] = gram[n : n + 1]

    def form(left, right):
        total = None
        for i, a in enumerate(left):
            if a is None:
                continue
            inner = None
            for j, b in enumerate(right):
                if b is None:
                    continue
                term = G[i, j] * b
                inner = term if inner is None else inner + term
            term = a * inner
            total = term if total is None else total + term
        return total

    def add(a, b):
        return b if a is None else (a if b is None else a + b)

    one = jnp.ones_like(m0)
    center = mu + DAMPING
    residual = [one, None, None, None, None]
    direction = list(residual)
    update = [None] * 5
    rr = G[0, 0]
    for turn in range(ITERS):
        image = [None] * 5
        for k in range(4):
            d = direction[k]
            if d is None:
                continue
            image[k] = add(image[k], center * d)
            image[k + 1] = add(image[k + 1], sigma * d)
            if k:
                image[k - 1] = add(image[k - 1], sigma * d)
        alpha = rr / form(direction, image)
        update = [add(u, None if d is None else alpha * d) for u, d in zip(update, direction)]
        residual = [add(r, None if q is None else -(alpha * q)) for r, q in zip(residual, image)]
        if turn < ITERS - 1:
            new = form(residual, residual)
            beta = new / rr
            direction = [add(r, None if d is None else beta * d) for r, d in zip(residual, direction)]
            rr = new
    for coords, out in ((update, upd_out), (residual, res_out)):
        for i in range(2):
            total = None
            for k in range(5):
                if coords[k] is not None:
                    term = coords[k] * basis[k][i]
                    total = term if total is None else total + term
            for j in range(2):
                moved = roll(total, -(32 + 16 * j))
                for c in range(3):
                    out[c, i, j : j + 1, :] = moved[c : c + 1, :9]

    for copy in (c_ylo, c_yhi, c_xlo, c_xhi, c_dlo, c_dhi, *kcopies, *rcopies, *vcopies):
        copy.wait_send()
    for which, (slots_a, slots_b) in enumerate(((a1, b1), (a2, b2))):
        pltpu.make_async_copy(slots_a.at[pl.ds(0, NGY - 1)], slots_a.at[pl.ds(0, NGY - 1)], arsem_s.at[which, 0]).wait()
        pltpu.make_async_copy(slots_b.at[pl.ds(0, NGX - 1)], slots_b.at[pl.ds(0, NGX - 1)], arsem_s.at[which, 1]).wait()


def local(reference_scan, deformed_scan, source_column):
    table = source_column.reshape(NGY, 1, 64)
    consts = constants()
    vmem = pl.BlockSpec(memory_space=pltpu.VMEM)
    hbm = pl.BlockSpec(memory_space=pl.ANY)
    V, DMA = pltpu.VMEM, pltpu.SemaphoreType.DMA
    scratch = [
        V((32, 32, 128), BF16), V((32, 32, 128), BF16), V((32, 32, 128), BF16), V((32, 32, 128), BF16),
        V((34, 48, 128), F32), V((3, 32, 32, 128), F32), V((16, 128), F32),
        V((2, 32, 128), BF16), V((32, 128), BF16), V((32, 128), BF16), V((32, 128), BF16), V((32, 128), BF16),
        V((5, 192, 128), F32), V((48, 640), F32), V((4, 5, 8, 128), F32), V((3, 4, 5, 8, 128), F32),
        V((3, 96, 128), F32), V((32, 384), F32), V((3, 8, 128), F32), V((4, 4, 3, 8, 128), F32),
        V((9, 9, 8, 128), F32), V((640, 512), BF16), V((2, 8, 128), F32), V((3, 3, 2, 8, 128), F32),
        V((8, 128), F32), V((NGY, 8, 128), F32), V((8, 128), F32), V((NGX, 8, 128), F32),
        V((16, 128), F32), V((NGY, 16, 128), F32), V((16, 128), F32), V((NGX, 16, 128), F32),
        DMA((3,)), DMA((6,)), DMA((6,)), DMA((8,)), DMA((8,)), DMA((15,)), DMA((15,)), DMA((8,)), DMA((8,)),
        DMA((2, 2)), DMA((2, 2)),
    ]
    out = jax.ShapeDtypeStruct((3, 2, 2, 9), F32)
    return pl.pallas_call(
        kernel,
        out_shape=(out, out),
        in_specs=[hbm, hbm, vmem, vmem, hbm, vmem, vmem, vmem, vmem],
        out_specs=(vmem, vmem),
        scratch_shapes=scratch,
        compiler_params=pltpu.CompilerParams(
            collective_id=0, has_side_effects=True, vmem_limit_bytes=40 * 1024 * 1024
        ),
    )(reference_scan, deformed_scan, table, *consts)


def solution(mesh):
    return jax.shard_map(
        local,
        mesh=mesh,
        in_specs=(P("gx", "gy", None), P("gx", "gy", None), P("gx", None, None, None)),
        out_specs=(P(None, "gx", "gy", None), P(None, "gx", "gy", None)),
        check_vma=False,
    )
```

```python
import functools

import jax
import jax.numpy as jnp
import ml_dtypes
import numpy as np
from jax import lax
from jax.experimental import pallas as pl
from jax.experimental.pallas import tpu as pltpu
from jax.sharding import PartitionSpec as P

MESH = pl.DeviceIdType.MESH
E = 16
ITERS = 4
DAMPING = 0.1
NGX, NGY = 8, 32
F32, BF16 = jnp.float32, jnp.bfloat16

NEIGHBOURS = [(dx, dy) for dx in (-1, 0, 1) for dy in (-1, 0, 1) if (dx, dy) != (0, 0)]
SOURCES = [(bx, by) for bx in (-2, -1, 0, 1) for by in (-2, -1, 0, 1) if (bx, by) != (0, 0)]
PAIRS = [(0, 0), (1, 1), (2, 2), (0, 1), (1, 2), (2, 0)]


def hat(position):
    return np.maximum(0.0, 1.0 - np.abs(position) / E)


def chain(count, nodes):
    position = np.arange(count)
    w = np.stack([hat(position - E * n) for n in range(nodes)])
    out = []
    for n in range(nodes):
        out.append(w[n] * w[n])
        if n + 1 < nodes:
            out.append(w[n] * w[n + 1])
    return w, np.stack(out)


def constants():
    wy, cy = chain(32, 3)
    wz, cz = chain(128, 9)
    scale = 1.0 / 1024.0
    ymat = np.zeros((48, 192))
    for m in range(5):
        for p in range(6):
            ymat[m * 8 + p, p * 32 : (p + 1) * 32] = cy[m] * scale
    zd, zf = np.zeros((128, 16)), np.zeros((128, 16))
    zd[:, :9] = cz[0::2].T
    zf[:, :8] = cz[1::2].T
    wmat = np.zeros((5, 128, 4, 8, 16))
    D0, F0, D1, F1, D2 = range(5)
    place = {
        (0, 0): (F0, zd), (0, 1): (F1, zd), (0, 2): (D1, zd), (0, 3): (D2, zd),
        (0, 4): (F0, zf), (0, 5): (F1, zf), (0, 6): (D1, zf), (0, 7): (D2, zf),
        (1, 2): (D0, zd), (1, 3): (D1, zd), (1, 4): (D2, zd), (1, 5): (F0, zd), (1, 6): (F1, zd),
        (2, 2): (D0, zf), (2, 3): (D1, zf), (2, 4): (D2, zf), (2, 5): (F0, zf), (2, 6): (F1, zf),
        (3, 4): (D0, zd), (3, 5): (F0, zd), (3, 6): (D0, zf), (3, 7): (F0, zf),
    }
    for (group, block), (m, z) in place.items():
        wmat[m, :, group, block, :] = z
    wmat = wmat.reshape(640, 512)
    yr = np.zeros((32, 96))
    for n in range(3):
        for r in range(8):
            c = r % 3
            yr[n * 8 + r, c * 32 : (c + 1) * 32] = wy[n] / 32.0
    wr = np.zeros((3, 128, 8, 16))
    for n in range(3):
        wr[n, :, 2 + n, :9] = wz.T
    wr = wr.reshape(384, 128)
    dz = np.zeros((128, 128))
    for z in range(128):
        if z + 1 < 128:
            dz[z + 1, z] = 1.0
        if z > 0:
            dz[z - 1, z] = -1.0
    lanes = np.arange(128)
    spread = (np.arange(64)[:, None] % 4 == lanes[None, :] // 32).astype(np.float64)
    cast = lambda a: a.astype(ml_dtypes.bfloat16)
    return [cast(a) for a in (ymat, wmat, yr, wr, dz, spread)]


def pieces(x):
    hi = x.astype(BF16)
    rest = x - hi.astype(F32)
    mid = rest.astype(BF16)
    low = (rest - mid.astype(F32)).astype(BF16)
    return hi, mid, low


def two_sum(a, b):
    s = a + b
    t = s - a
    return s, (a - (s - t)) + (b - t)


def split(a):
    t = a * 4097.0
    high = t - (t - a)
    return high, a - high


def two_prod(a, a_halves, b, b_halves):
    p = a * b
    (ah, al), (bh, bl) = a_halves, b_halves
    return p, ((ah * bh - p) + ah * bl + al * bh) + al * bl


def add(a, b):
    return b if a is None else (a if b is None else a + b)


def mm(a, b):
    return jnp.dot(a, b, preferred_element_type=F32)


def kernel(
    ref_h, def_h, table_h, ymat_h, wmat_h, yr_h, wr_h, dz_h, spread_h,
    upd_out, res_out,
    table, ymat, yr, wr, dz, spread,
    ref_v, own_v, lo_v, hi_v, fs, gs, mask_s, yface, xlo, xhi, ylo, yhi,
    xs, t2, ksend, krecv, rx, rt2, rsend, rrecv, kf, wmat, vsend, vrecv,
    asrc, a1, b1src, b1,
    lsem, fsend, frecv, ksem_s, ksem_r, rsem_s, rsem_r, vsem_s, vsem_r, arsem_s, arsem_r,
):
    gx, gy = lax.axis_index("gx"), lax.axis_index("gy")

    def at(dx, dy):
        return (lax.rem(gx + (dx + NGX), NGX), lax.rem(gy + (dy + NGY), NGY))

    barrier = pltpu.get_barrier_semaphore()
    partners = [at(0, m) for m in range(1, NGY)] + [at(m, 0) for m in range(1, NGX)]
    partners += [at(bx, by) for bx, by in SOURCES if bx != 0 and by != 0]
    for partner in partners:
        pl.semaphore_signal(barrier, inc=1, device_id=partner, device_id_type=MESH)

    load_ref = pltpu.make_async_copy(ref_h, ref_v, lsem.at[0])
    load_own = pltpu.make_async_copy(def_h, own_v, lsem.at[1])
    load_w = pltpu.make_async_copy(wmat_h, wmat, lsem.at[2])
    small = [(table_h.at[gy], table), (spread_h, spread), (dz_h, dz), (ymat_h, ymat), (yr_h, yr), (wr_h, wr)]
    small = [pltpu.make_async_copy(src, dst, lsem.at[3 + n]) for n, (src, dst) in enumerate(small)]
    for copy in (load_ref, *small, load_own, load_w):
        copy.start()

    def flag(condition):
        return jnp.where(condition, 1.0, 0.0).astype(F32)

    xlo_ok, xhi_ok = flag(gx > 0), flag(gx < NGX - 1)
    ylo_ok, yhi_ok = flag(gy > 0), flag(gy < NGY - 1)

    for copy in small:
        copy.wait()
    row = (table[...] - gy).astype(F32)
    r16 = lax.broadcasted_iota(jnp.int32, (16, 64), 0)
    c64 = lax.broadcasted_iota(jnp.int32, (16, 64), 1)
    picked = jnp.where(c64 // 4 == r16, jnp.broadcast_to(row, (16, 64)), 0.0).astype(BF16)
    mask_s[...] = mm(picked, spread[...])

    load_ref.wait()
    for x in range(32):
        plane = ref_v[x]
        fs[x + 1, 8:40, :] = plane.astype(F32)
        gs[2, x] = mm(plane, dz[...])
    yface[0] = jnp.concatenate([fs[x + 1, 39:40, :] for x in range(32)], axis=0).astype(BF16)
    yface[1] = jnp.concatenate([fs[x + 1, 8:9, :] for x in range(32)], axis=0).astype(BF16)

    pl.semaphore_wait(barrier, len(partners))

    def send(src, dst, s, r, to):
        copy = pltpu.make_async_remote_copy(
            src_ref=src, dst_ref=dst, send_sem=s, recv_sem=r, device_id=to, device_id_type=MESH
        )
        copy.start()
        return copy

    c_ylo = send(yface.at[0], ylo, fsend.at[0], frecv.at[0], at(0, 1))
    c_yhi = send(yface.at[1], yhi, fsend.at[1], frecv.at[1], at(0, -1))
    c_xlo = send(ref_v.at[31], xlo, fsend.at[2], frecv.at[2], at(1, 0))
    c_xhi = send(ref_v.at[0], xhi, fsend.at[3], frecv.at[3], at(-1, 0))
    load_own.wait()
    c_dlo = send(own_v, lo_v, fsend.at[4], frecv.at[4], at(0, 1))
    c_dhi = send(own_v, hi_v, fsend.at[5], frecv.at[5], at(0, -1))
    c_xlo.wait_recv()
    c_xhi.wait_recv()
    c_ylo.wait_recv()
    c_yhi.wait_recv()
    fs[0, 8:40, :] = xlo[...].astype(F32) * xlo_ok
    fs[33, 8:40, :] = xhi[...].astype(F32) * xhi_ok
    face_lo = ylo[...].astype(F32) * ylo_ok
    face_hi = yhi[...].astype(F32) * yhi_ok
    for x in range(32):
        fs[x + 1, 7:8, :] = face_lo[x : x + 1]
        fs[x + 1, 40:41, :] = face_hi[x : x + 1]

    for ey in range(2):
        r = 8 + 16 * ey
        y = slice(16 * ey, 16 * ey + 16)
        moments = []
        for ex in range(2):
            def step(t, carry, ex=ex, r=r, y=y):
                x = 16 * ex + t
                g = (
                    fs[x + 2, r : r + 16, :] - fs[x, r : r + 16, :],
                    fs[x + 1, r + 1 : r + 17, :] - fs[x + 1, r - 1 : r + 15, :],
                    gs[2, x, y, :],
                )
                gs[0, x, y, :] = g[0]
                gs[1, x, y, :] = g[1]
                out = []
                for p, (c, d) in enumerate(PAIRS):
                    s1, s2, s3 = carry[p]
                    s1 = s1 + g[c] * g[d]
                    s2 = s2 + s1
                    s3 = s3 + s2
                    out.append((s1, s2, s3))
                return tuple(out)

            zero = jnp.zeros((16, 128), F32)
            sums = lax.fori_loop(0, 16, step, tuple((zero,) * 3 for _ in PAIRS), unroll=4)
            weighted = []
            for s1, s2, s3 in sums:
                m00 = (2.0 * s3 - s2) * (1.0 / 256.0)
                first = s2 * (1.0 / 16.0)
                weighted.append((m00, first - m00, s1 - 2.0 * first + m00))
            moments.append(weighted)
        for p in range(6):
            (a00, a01, a11), (b00, b01, b11) = moments[0][p], moments[1][p]
            rows = slice(p * 32 + 16 * ey, p * 32 + 16 * ey + 16)
            for u, value in enumerate((a00, a01, a11 + b00, b01, b11)):
                xs[u, rows, :] = value

    t2[40:48, :] = jnp.zeros((8, 640), F32)
    for u in range(5):
        hi, mid, low = pieces(xs[u])
        t = mm(ymat[...], hi) + mm(ymat[...], mid) + mm(ymat[...], low)
        for m in range(5):
            t2[8 * u : 8 * u + 8, 128 * m : 128 * m + 128] = t[8 * m : 8 * m + 8]
    load_w.wait()
    stacked = jnp.concatenate(pieces(t2[...]), axis=0)
    done = mm(stacked, wmat[...])
    done = done[:48] + done[48:96] + done[96:144]
    for u in range(5):
        for group in range(4):
            ksend[group, u] = done[8 * u : 8 * u + 8, 128 * group : 128 * group + 128]

    GROUP = {1: (0, 1), 0: (1, 2), -1: (3, 1)}
    UNIT = {1: (1, 4), 0: (0, 5), -1: (0, 2)}
    kcopies = []
    for n, (dx, dy) in enumerate(NEIGHBOURS):
        g0, gn = GROUP[dy]
        u0, un = UNIT[dx]
        kcopies.append(
            send(
                ksend.at[pl.ds(g0, gn), pl.ds(u0, un)],
                krecv.at[1 - dx, pl.ds(g0, gn), pl.ds(u0, un)],
                ksem_s.at[n], ksem_r.at[n], at(dx, dy),
            )
        )
    krecv[1, 1:3] = ksend[1:3]

    c_dlo.wait_recv()
    c_dhi.wait_recv()
    for ey in range(2):
        r = 8 + 16 * ey
        y = slice(16 * ey, 16 * ey + 16)
        parts = []
        for ex in range(2):
            carry = tuple((jnp.zeros((16, 128), F32),) * 2 for _ in range(3))
            for xb in range(2):
                k = (2 * ex + xb) * 4 + 2 * ey
                off = jnp.concatenate(
                    [jnp.broadcast_to(mask_s[k + h : k + h + 1, :], (8, 128)) for h in range(2)], axis=0
                )
                below, above = off < -0.5, off > 0.5

                def step(t, carry, below=below, above=above, ex=ex, xb=xb, r=r, y=y):
                    x = 16 * ex + 8 * xb + t
                    warped = jnp.where(
                        below, lo_v[x, y, :].astype(F32),
                        jnp.where(above, hi_v[x, y, :].astype(F32), own_v[x, y, :].astype(F32)),
                    )
                    misfit = fs[x + 1, r : r + 16, :] - warped
                    out = []
                    for c in range(3):
                        s1, s2 = carry[c]
                        s1 = s1 + gs[c, x, y, :] * misfit
                        out.append((s1, s2 + s1))
                    return tuple(out)

                carry = lax.fori_loop(0, 8, step, carry, unroll=4)
            parts.append([(s2 * (1.0 / 16.0), s1 - s2 * (1.0 / 16.0)) for s1, s2 in carry])
        for c in range(3):
            (a0, a1_), (b0, b1_) = parts[0][c], parts[1][c]
            rows = slice(c * 32 + 16 * ey, c * 32 + 16 * ey + 16)
            for n, value in enumerate((a0, a1_ + b0, b1_)):
                rx[n, rows, :] = value
    rt2[24:32, :] = jnp.zeros((8, 384), F32)
    for n in range(3):
        hi, mid, low = pieces(rx[n])
        t = mm(yr[...], hi) + mm(yr[...], mid) + mm(yr[...], low)
        for m in range(3):
            rt2[8 * n : 8 * n + 8, 128 * m : 128 * m + 128] = t[8 * m : 8 * m + 8]
    stacked = jnp.concatenate(pieces(rt2[...]), axis=0)
    done = mm(stacked, wr[...])
    done = done[:32] + done[32:64] + done[64:96]
    for n in range(3):
        rsend[n] = done[8 * n : 8 * n + 8]
    rcopies = []
    for n, (bx, by) in enumerate(SOURCES):
        rcopies.append(
            send(rsend, rrecv.at[bx + 2, by + 2], rsem_s.at[n], rsem_r.at[n], at(-bx, -by))
        )
    rrecv[2, 2] = rsend[...]

    lane = lax.broadcasted_iota(jnp.int32, (8, 128), 1)
    sub = lax.broadcasted_iota(jnp.int32, (8, 128), 0)
    slot, depth = lane // 16, lane % 16

    def roll(x, shift):
        shift = shift % 128
        return x if shift == 0 else pltpu.roll(x, shift, 1)

    for copy in kcopies:
        copy.wait_recv()
    in_a_diag = jnp.where(slot == 1, 1.0, jnp.where(slot == 2, ylo_ok, 0.0))
    in_b_diag = (slot >= 2) & (slot <= 4)
    for e in range(9):
        def entry(group, e=e):
            if e == 3:
                return krecv[0, group, 4] * xlo_ok + krecv[1, group, 0]
            if e == 7:
                return krecv[1, group, 4] + krecv[2, group, 0]
            if e < 3:
                return krecv[0, group, e + 1]
            if e < 7:
                return krecv[1, group, e - 3]
            return krecv[2, group, 1]

        a, b0, b1_, c = [entry(group) for group in range(4)]

        def diag(a, b, c):
            return a * in_a_diag + jnp.where(in_b_diag, b, 0.0) + jnp.where(slot == 4, c, 0.0)

        def off_diag(a, b, c):
            return jnp.where(slot < 2, a, jnp.where(slot < 4, b, jnp.where(slot == 4, c, 0.0)))

        dd = diag(roll(a, -16), b0, c)
        fd = off_diag(a, roll(b0, -48), roll(c, -16))
        df = diag(roll(a, -80), b1_, roll(c, -32))
        ff = off_diag(roll(a, -64), roll(b1_, -48), roll(c, -48))
        kf[e, 4] = dd
        kf[e, 5] = df
        kf[e, 3] = roll(df, 1)
        kf[e, 7] = fd
        kf[e, 1] = roll(fd, 16)
        kf[e, 8] = ff
        kf[e, 6] = roll(ff, 1)
        kf[e, 2] = roll(ff, 16)
        kf[e, 0] = roll(ff, 17)

    lane_j = 2 * gy + slot - 2
    lane_ok = (lane_j >= 0) & (lane_j < 64) & (slot < 6) & (depth < 9)
    lane_mask = jnp.where(lane_ok, 1.0, 0.0)
    node_mask = {i: lane_mask * flag((2 * gx + i >= 0) & (2 * gx + i < 16)) for i in range(-2, 4)}
    own_mask = jnp.where((slot >= 2) & (slot < 4) & (depth < 9), 1.0, 0.0)

    def apply(v, rows):
        need = sorted({i + ox for i in rows for ox in (-1, 0, 1)})
        first, second = {}, {}
        for i in need:
            second[i] = v[i]
            first[i] = jnp.where(sub < 3, v[i], pltpu.roll(v[i], 7, 0))
        acc1 = {i: jnp.zeros((8, 128), F32) for i in rows}
        acc2 = {i: jnp.zeros((8, 128), F32) for i in rows}
        for o in range(9):
            oy, oz = o // 3 - 1, o % 3 - 1
            s1 = {i: roll(first[i], -(16 * oy + oz)) for i in need}
            s2 = {i: roll(second[i], -(16 * oy + oz)) for i in need}
            for i in rows:
                for ox in (-1, 0, 1):
                    k = kf[2 * i + 3 + ox, o]
                    acc1[i] = acc1[i] + k * s1[i + ox]
                    acc2[i] = acc2[i] + k * s2[i + ox]
        out = {}
        for i in rows:
            total = acc1[i] + pltpu.roll(acc1[i], 5, 0)
            total = total + jnp.where(sub == 0, pltpu.roll(acc2[i], 3, 0), pltpu.roll(acc2[i], 6, 0))
            out[i] = jnp.where(sub < 3, total, jnp.where(sub < 6, pltpu.roll(total, 3, 0), pltpu.roll(total, 6, 0)))
        return out

    for copy in rcopies:
        copy.wait_recv()
    w0 = {}
    lo2_x, lo2_y = flag(gx > 1), flag(gy > 1)
    x_ok = {-2: lo2_x, -1: xlo_ok, 0: None, 1: None}
    y_ok = {-2: lo2_y, -1: ylo_ok, 0: None, 1: None}
    for i in range(-2, 4):
        total = None
        for by in (-2, -1, 0, 1):
            part = None
            for bx in (-2, -1, 0, 1):
                n = i - 2 * bx
                if 0 <= n <= 2:
                    term = rrecv[bx + 2, by + 2, n]
                    if x_ok[bx] is not None:
                        term = term * x_ok[bx]
                    part = term if part is None else part + term
            part = roll(part, 32 * by)
            if y_ok[by] is not None:
                part = part * y_ok[by]
            total = part if total is None else total + part
        w0[i] = total * node_mask[i]

    w1 = apply(w0, (-1, 0, 1, 2))
    w1 = {i: w1[i] * node_mask[i] for i in w1}
    w2_own = apply(w1, (0, 1))
    for i in range(2):
        vsend[i] = w2_own[i] * own_mask
    vcopies = []
    for n, (dx, dy) in enumerate(NEIGHBOURS):
        vcopies.append(
            send(vsend, vrecv.at[1 - dx, 1 - dy], vsem_s.at[n], vsem_r.at[n], at(dx, dy))
        )
    vrecv[1, 1] = vsend[...]

    for copy in vcopies:
        copy.wait_recv()
    w2 = {}
    for i in range(-2, 4):
        bx, n = i // 2, i % 2
        total = vrecv[bx + 1, 1, n] + roll(vrecv[bx + 1, 0, n], -32) + roll(vrecv[bx + 1, 2, n], 32)
        w2[i] = total * node_mask[i]
    w3 = apply(w2, (-1, 0, 1, 2))
    w3 = {i: w3[i] * node_mask[i] for i in w3}
    w4 = apply(w3, (0, 1))
    krylov = [w0, w1, w2, w3, w4]

    packed = [jnp.where(sub < 3, w[0], jnp.where(sub < 6, w[1], 0.0)) * own_mask for w in krylov]
    left = roll(packed[0], -32) + packed[1] + roll(packed[2], 32) + roll(packed[3], 64)
    left_halves = split(left)
    value = remainder = jnp.zeros((8, 128), F32)
    for j in range(5):
        right = packed[j] + roll(packed[j], 32)
        right = right + roll(right, 64)
        p, e = two_prod(left, left_halves, right, split(right))
        for shift in (4, 2, 1):
            p, err = two_sum(p, pltpu.roll(p, shift, 0))
            e = e + pltpu.roll(e, shift, 0) + err
        value = jnp.where(sub == j, p, value)
        remainder = jnp.where(sub == j, e, remainder)

    def pair_tree(slots):
        p, e = slots[:, 0], slots[:, 1]
        while p.shape[0] > 1:
            half = p.shape[0] // 2
            e = e[:half] + e[half:]
            p, err = two_sum(p[:half], p[half:])
            e = e + err
        return p[0], e[0]

    asrc[0] = value
    asrc[1] = remainder
    a1[gy] = asrc[...]
    for m in range(1, NGY):
        send(asrc, a1.at[gy], arsem_s.at[0], arsem_r.at[0], at(0, m))
    pltpu.make_async_copy(a1.at[pl.ds(0, NGY - 1)], a1.at[pl.ds(0, NGY - 1)], arsem_r.at[0]).wait()
    p, e = pair_tree(a1[...])
    b1src[0] = p
    b1src[1] = e
    b1[gx] = b1src[...]
    for m in range(1, NGX):
        send(b1src, b1.at[gx], arsem_s.at[1], arsem_r.at[1], at(m, 0))
    pltpu.make_async_copy(b1.at[pl.ds(0, NGX - 1)], b1.at[pl.ds(0, NGX - 1)], arsem_r.at[1]).wait()
    p, e = pair_tree(b1[...])
    for shift in (16, 8, 4, 2, 1):
        e = e + roll(e, -shift)
        p, err = two_sum(p, roll(p, -shift))
        e = e + err
    high = p + e
    low = (p - high) + e

    def few_bits(x):
        t = x * 262145.0
        return t - (t - x)

    m0, m1, m2 = high[0:1, 0:1], high[1:2, 0:1], high[1:2, 32:33]
    mean = m1 / m0
    mu = few_bits(mean)
    spread_q = few_bits(jnp.maximum(m2 / m0 - mean * mean, 1e-5 * mean * mean))
    poly = [[jnp.ones_like(m0)]]
    for k in range(4):
        new = [None] + list(poly[k])
        for i, a in enumerate(poly[k]):
            new[i] = add(new[i], -(mu * a))
        if k:
            for i, a in enumerate(poly[k - 1]):
                new[i] = new[i] - spread_q * a
        poly.append(new)

    def combine(coefficients, terms):
        total = None
        for c, (h, l) in zip(coefficients, terms):
            c = jnp.broadcast_to(c, h.shape)
            p, e = two_prod(c, split(c), h, split(h))
            e = e + c * l
            if total is None:
                total = (p, e)
            else:
                q, err = two_sum(total[0], p)
                total = (q, total[1] + e + err)
        h = total[0] + total[1]
        return h, (total[0] - h) + total[1]

    rows_w = [(high[j : j + 1], low[j : j + 1]) for j in range(5)]
    rows_q = [combine(poly[k], rows_w) for k in range(5)]
    filler = [jnp.zeros((3, 128), F32)]
    mixed = [jnp.concatenate([r[n] for r in rows_q] + filler, axis=0) for n in range(2)]
    moved = [tuple(roll(x, -32 * t) for x in mixed) for t in range(4)]
    G = {}
    for l in range(4):
        h, _ = combine(poly[l], moved)
        for k in range(l, 5):
            G[k, l] = G[l, k] = h[k : k + 1, 0:1]

    own = (0, 1)

    def times(k_of, v, older):
        return {i: k_of[i] - mu * v[i] - (0.0 if older is None else spread_q * older[i]) for i in own}

    q1 = times(w1, w0, None)
    kq1 = times(w2, w1, None)
    kkq1 = times(w3, w2, None)
    kkkq1 = times(w4, w3, None)
    q2 = times(kq1, q1, w0)
    kq2 = times(kkq1, kq1, w1)
    kkq2 = times(kkkq1, kkq1, w2)
    q3 = times(kq2, q2, q1)
    kq3 = times(kkq2, kq2, kq1)
    q4 = times(kq3, q3, q2)
    basis = [w0, q1, q2, q3, q4]

    def form(left, right):
        total = None
        for i, a in enumerate(left):
            if a is None:
                continue
            inner = None
            for j, b in enumerate(right):
                if b is None:
                    continue
                term = G[i, j] * b
                inner = term if inner is None else inner + term
            term = a * inner
            total = term if total is None else total + term
        return total

    one = jnp.ones_like(m0)
    center = mu + DAMPING
    residual = [one, None, None, None, None]
    direction = list(residual)
    update = [None] * 5
    rr = G[0, 0]
    for turn in range(ITERS):
        image = [None] * 5
        for k in range(4):
            d = direction[k]
            if d is None:
                continue
            image[k] = add(image[k], center * d)
            image[k + 1] = add(image[k + 1], d)
            if k:
                image[k - 1] = add(image[k - 1], spread_q * d)
        alpha = rr / form(direction, image)
        update = [add(u, None if d is None else alpha * d) for u, d in zip(update, direction)]
        residual = [add(r, None if q is None else -(alpha * q)) for r, q in zip(residual, image)]
        if turn < ITERS - 1:
            new = form(residual, residual)
            beta = new / rr
            direction = [add(r, None if d is None else beta * d) for r, d in zip(residual, direction)]
            rr = new
    for coords, out in ((update, upd_out), (residual, res_out)):
        for i in range(2):
            total = None
            for k in range(5):
                if coords[k] is not None:
                    term = coords[k] * basis[k][i]
                    total = term if total is None else total + term
            for j in range(2):
                moved = roll(total, -(32 + 16 * j))
                for c in range(3):
                    out[c, i, j : j + 1, :] = moved[c : c + 1, :9]

    for copy in (c_ylo, c_yhi, c_xlo, c_xhi, c_dlo, c_dhi, *kcopies, *rcopies, *vcopies):
        copy.wait_send()
    pltpu.make_async_copy(a1.at[pl.ds(0, NGY - 1)], a1.at[pl.ds(0, NGY - 1)], arsem_s.at[0]).wait()
    pltpu.make_async_copy(b1.at[pl.ds(0, NGX - 1)], b1.at[pl.ds(0, NGX - 1)], arsem_s.at[1]).wait()


def local(reference_scan, deformed_scan, source_column):
    table = source_column.reshape(NGY, 1, 64)
    consts = constants()
    vmem = pl.BlockSpec(memory_space=pltpu.VMEM)
    hbm = pl.BlockSpec(memory_space=pltpu.HBM)
    V, DMA = pltpu.VMEM, pltpu.SemaphoreType.DMA
    scratch = [
        V((1, 64), jnp.int32), V((48, 192), BF16), V((32, 96), BF16), V((384, 128), BF16), V((128, 128), BF16), V((64, 128), BF16),
        V((32, 32, 128), BF16), V((32, 32, 128), BF16), V((32, 32, 128), BF16), V((32, 32, 128), BF16),
        V((34, 48, 128), F32), V((3, 32, 32, 128), F32), V((16, 128), F32),
        V((2, 32, 128), BF16), V((32, 128), BF16), V((32, 128), BF16), V((32, 128), BF16), V((32, 128), BF16),
        V((5, 192, 128), F32), V((48, 640), F32), V((4, 5, 8, 128), F32), V((3, 4, 5, 8, 128), F32),
        V((3, 96, 128), F32), V((32, 384), F32), V((3, 8, 128), F32), V((4, 4, 3, 8, 128), F32),
        V((9, 9, 8, 128), F32), V((640, 512), BF16), V((2, 8, 128), F32), V((3, 3, 2, 8, 128), F32),
        V((2, 8, 128), F32), V((NGY, 2, 8, 128), F32), V((2, 8, 128), F32), V((NGX, 2, 8, 128), F32),
        DMA((9,)), DMA((6,)), DMA((6,)), DMA((8,)), DMA((8,)), DMA((15,)), DMA((15,)), DMA((8,)), DMA((8,)),
        DMA((2,)), DMA((2,)),
    ]
    out = jax.ShapeDtypeStruct((3, 2, 2, 9), F32)
    return pl.pallas_call(
        kernel,
        out_shape=(out, out),
        in_specs=[hbm] * 9,
        out_specs=(vmem, vmem),
        scratch_shapes=scratch,
        compiler_params=pltpu.CompilerParams(
            collective_id=0, has_side_effects=True, vmem_limit_bytes=40 * 1024 * 1024
        ),
    )(reference_scan, deformed_scan, table, *consts)


def solution(mesh):
    return jax.shard_map(
        local,
        mesh=mesh,
        in_specs=(P("gx", "gy", None), P("gx", "gy", None), P("gx", None, None, None)),
        out_specs=(P(None, "gx", "gy", None), P(None, "gx", "gy", None)),
        check_vma=False,
    )
```

```python
import functools

import jax
import jax.numpy as jnp
import ml_dtypes
import numpy as np
from jax import lax
from jax.experimental import pallas as pl
from jax.experimental.pallas import tpu as pltpu
from jax.sharding import PartitionSpec as P

MESH = pl.DeviceIdType.MESH
E = 16
ITERS = 4
DAMPING = 0.1
NGX, NGY = 8, 32
F32, BF16 = jnp.float32, jnp.bfloat16

NEIGHBOURS = [(dx, dy) for dx in (-1, 0, 1) for dy in (-1, 0, 1) if (dx, dy) != (0, 0)]
SOURCES = [(bx, by) for bx in (-2, -1, 0, 1) for by in (-2, -1, 0, 1) if (bx, by) != (0, 0)]
PAIRS = [(0, 0), (1, 1), (2, 2), (0, 1), (1, 2), (2, 0)]


def hat(position):
    return np.maximum(0.0, 1.0 - np.abs(position) / E)


def chain(count, nodes):
    position = np.arange(count)
    w = np.stack([hat(position - E * n) for n in range(nodes)])
    out = []
    for n in range(nodes):
        out.append(w[n] * w[n])
        if n + 1 < nodes:
            out.append(w[n] * w[n + 1])
    return w, np.stack(out)


def constants():
    wy, cy = chain(32, 3)
    wz, cz = chain(128, 9)
    scale = 1.0 / 1024.0
    ymat = np.zeros((48, 192))
    for m in range(5):
        for p in range(6):
            ymat[m * 8 + p, p * 32 : (p + 1) * 32] = cy[m] * scale
    zd, zf = np.zeros((128, 16)), np.zeros((128, 16))
    zd[:, :9] = cz[0::2].T
    zf[:, :8] = cz[1::2].T
    wmat = np.zeros((5, 128, 4, 8, 16))
    D0, F0, D1, F1, D2 = range(5)
    place = {
        (0, 0): (F0, zd), (0, 1): (F1, zd), (0, 2): (D1, zd), (0, 3): (D2, zd),
        (0, 4): (F0, zf), (0, 5): (F1, zf), (0, 6): (D1, zf), (0, 7): (D2, zf),
        (1, 2): (D0, zd), (1, 3): (D1, zd), (1, 4): (D2, zd), (1, 5): (F0, zd), (1, 6): (F1, zd),
        (2, 2): (D0, zf), (2, 3): (D1, zf), (2, 4): (D2, zf), (2, 5): (F0, zf), (2, 6): (F1, zf),
        (3, 4): (D0, zd), (3, 5): (F0, zd), (3, 6): (D0, zf), (3, 7): (F0, zf),
    }
    for (group, block), (m, z) in place.items():
        wmat[m, :, group, block, :] = z
    wmat = wmat.reshape(640, 512)
    yr = np.zeros((32, 96))
    for n in range(3):
        for r in range(8):
            c = r % 3
            yr[n * 8 + r, c * 32 : (c + 1) * 32] = wy[n] / 32.0
    wr = np.zeros((3, 128, 8, 16))
    for n in range(3):
        wr[n, :, 2 + n, :9] = wz.T
    wr = wr.reshape(384, 128)
    dz = np.zeros((128, 128))
    for z in range(128):
        if z + 1 < 128:
            dz[z + 1, z] = 1.0
        if z > 0:
            dz[z - 1, z] = -1.0
    lanes = np.arange(128)
    spread = (np.arange(64)[:, None] % 4 == lanes[None, :] // 32).astype(np.float64)
    cast = lambda a: a.astype(ml_dtypes.bfloat16)
    both = np.zeros((80, 192))
    both[:48] = ymat
    both[48:, :96] = yr
    return [cast(a) for a in (both, wmat, wr, dz, spread)]


def pieces(x):
    hi = x.astype(BF16)
    rest = x - hi.astype(F32)
    mid = rest.astype(BF16)
    low = (rest - mid.astype(F32)).astype(BF16)
    return hi, mid, low


def two_sum(a, b):
    s = a + b
    t = s - a
    return s, (a - (s - t)) + (b - t)


def split(a):
    t = a * 4097.0
    high = t - (t - a)
    return high, a - high


def two_prod(a, a_halves, b, b_halves):
    p = a * b
    (ah, al), (bh, bl) = a_halves, b_halves
    return p, ((ah * bh - p) + ah * bl + al * bh) + al * bl


def add(a, b):
    return b if a is None else (a if b is None else a + b)


def mm(a, b):
    return jnp.dot(a, b, preferred_element_type=F32)


def kernel(
    ref_h, def_h, table_h, ys_h, wmat_h, wr_h, dz_h, spread_h,
    upd_out, res_out,
    table, ys, wr, dz, spread,
    ref_v, own_v, lo_v, hi_v, fs, gs, mask_s, yface, xlo, xhi, ylo, yhi,
    xs, t2, ksend, krecv, rx, rt2, rsend, rrecv, kf, wmat, vsend, vrecv,
    asrc, a1, b1src, b1,
    lsem, fsend, frecv, ksem_s, ksem_r, rsem_s, rsem_r, vsem_s, vsem_r, arsem_s, arsem_r,
):
    gx, gy = lax.axis_index("gx"), lax.axis_index("gy")

    def at(dx, dy):
        return (lax.rem(gx + (dx + NGX), NGX), lax.rem(gy + (dy + NGY), NGY))

    barrier = pltpu.get_barrier_semaphore()
    partners = [at(0, m) for m in range(1, NGY)] + [at(m, 0) for m in range(1, NGX)]
    partners += [at(bx, by) for bx, by in SOURCES if bx != 0 and by != 0]
    for partner in partners:
        pl.semaphore_signal(barrier, inc=1, device_id=partner, device_id_type=MESH)

    load_ref = pltpu.make_async_copy(ref_h, ref_v, lsem.at[0])
    load_own = pltpu.make_async_copy(def_h, own_v, lsem.at[1])
    load_w = pltpu.make_async_copy(wmat_h, wmat, lsem.at[2])
    small = [(table_h.at[gy], table), (spread_h, spread), (dz_h, dz), (ys_h, ys), (wr_h, wr)]
    small = [pltpu.make_async_copy(src, dst, lsem.at[3 + n]) for n, (src, dst) in enumerate(small)]
    for copy in (load_ref, *small, load_own, load_w):
        copy.start()

    def flag(condition):
        return jnp.where(condition, 1.0, 0.0).astype(F32)

    xlo_ok, xhi_ok = flag(gx > 0), flag(gx < NGX - 1)
    ylo_ok, yhi_ok = flag(gy > 0), flag(gy < NGY - 1)

    for copy in small:
        copy.wait()
    row = (table[...] - gy).astype(F32)
    r16 = lax.broadcasted_iota(jnp.int32, (16, 64), 0)
    c64 = lax.broadcasted_iota(jnp.int32, (16, 64), 1)
    picked = jnp.where(c64 // 4 == r16, jnp.broadcast_to(row, (16, 64)), 0.0).astype(BF16)
    mask_s[...] = mm(picked, spread[...])

    load_ref.wait()
    for x in range(32):
        plane = ref_v[x]
        fs[x + 1, 8:40, :] = plane.astype(F32)
        gs[2, x] = mm(plane, dz[...])
    yface[0] = jnp.concatenate([fs[x + 1, 39:40, :] for x in range(32)], axis=0).astype(BF16)
    yface[1] = jnp.concatenate([fs[x + 1, 8:9, :] for x in range(32)], axis=0).astype(BF16)

    pl.semaphore_wait(barrier, len(partners))

    def send(src, dst, s, r, to):
        copy = pltpu.make_async_remote_copy(
            src_ref=src, dst_ref=dst, send_sem=s, recv_sem=r, device_id=to, device_id_type=MESH
        )
        copy.start()
        return copy

    c_ylo = send(yface.at[0], ylo, fsend.at[0], frecv.at[0], at(0, 1))
    c_yhi = send(yface.at[1], yhi, fsend.at[1], frecv.at[1], at(0, -1))
    c_xlo = send(ref_v.at[31], xlo, fsend.at[2], frecv.at[2], at(1, 0))
    c_xhi = send(ref_v.at[0], xhi, fsend.at[3], frecv.at[3], at(-1, 0))
    load_own.wait()
    c_dlo = send(own_v, lo_v, fsend.at[4], frecv.at[4], at(0, 1))
    c_dhi = send(own_v, hi_v, fsend.at[5], frecv.at[5], at(0, -1))
    c_xlo.wait_recv()
    c_xhi.wait_recv()
    c_ylo.wait_recv()
    c_yhi.wait_recv()
    fs[0, 8:40, :] = xlo[...].astype(F32) * xlo_ok
    fs[33, 8:40, :] = xhi[...].astype(F32) * xhi_ok
    face_lo = ylo[...].astype(F32) * ylo_ok
    face_hi = yhi[...].astype(F32) * yhi_ok
    for x in range(32):
        fs[x + 1, 7:8, :] = face_lo[x : x + 1]
        fs[x + 1, 40:41, :] = face_hi[x : x + 1]

    for ey in range(2):
        r = 8 + 16 * ey
        y = slice(16 * ey, 16 * ey + 16)
        moments = []
        for ex in range(2):
            def step(t, carry, ex=ex, r=r, y=y):
                x = 16 * ex + t
                g = (
                    fs[x + 2, r : r + 16, :] - fs[x, r : r + 16, :],
                    fs[x + 1, r + 1 : r + 17, :] - fs[x + 1, r - 1 : r + 15, :],
                    gs[2, x, y, :],
                )
                gs[0, x, y, :] = g[0]
                gs[1, x, y, :] = g[1]
                out = []
                for p, (c, d) in enumerate(PAIRS):
                    s1, s2, s3 = carry[p]
                    s1 = s1 + g[c] * g[d]
                    s2 = s2 + s1
                    s3 = s3 + s2
                    out.append((s1, s2, s3))
                return tuple(out)

            zero = jnp.zeros((16, 128), F32)
            sums = lax.fori_loop(0, 16, step, tuple((zero,) * 3 for _ in PAIRS), unroll=4)
            weighted = []
            for s1, s2, s3 in sums:
                m00 = (2.0 * s3 - s2) * (1.0 / 256.0)
                first = s2 * (1.0 / 16.0)
                weighted.append((m00, first - m00, s1 - 2.0 * first + m00))
            moments.append(weighted)
        for p in range(6):
            (a00, a01, a11), (b00, b01, b11) = moments[0][p], moments[1][p]
            rows = slice(p * 32 + 16 * ey, p * 32 + 16 * ey + 16)
            for u, value in enumerate((a00, a01, a11 + b00, b01, b11)):
                xs[u, rows, :] = value

    ymat = ys[:48, :]
    t2[40:48, :] = jnp.zeros((8, 640), F32)
    for u in range(5):
        hi, mid, low = pieces(xs[u])
        t = mm(ymat, hi) + mm(ymat, mid) + mm(ymat, low)
        for m in range(5):
            t2[8 * u : 8 * u + 8, 128 * m : 128 * m + 128] = t[8 * m : 8 * m + 8]
    load_w.wait()
    stacked = jnp.concatenate(pieces(t2[...]), axis=0)
    done = mm(stacked, wmat[...])
    done = done[:48] + done[48:96] + done[96:144]
    for u in range(5):
        for group in range(4):
            ksend[group, u] = done[8 * u : 8 * u + 8, 128 * group : 128 * group + 128]

    GROUP = {1: (0, 1), 0: (1, 2), -1: (3, 1)}
    UNIT = {1: (1, 4), 0: (0, 5), -1: (0, 2)}
    kcopies = []
    for n, (dx, dy) in enumerate(NEIGHBOURS):
        g0, gn = GROUP[dy]
        u0, un = UNIT[dx]
        kcopies.append(
            send(
                ksend.at[pl.ds(g0, gn), pl.ds(u0, un)],
                krecv.at[1 - dx, pl.ds(g0, gn), pl.ds(u0, un)],
                ksem_s.at[n], ksem_r.at[n], at(dx, dy),
            )
        )
    krecv[1, 1:3] = ksend[1:3]

    c_dlo.wait_recv()
    c_dhi.wait_recv()
    for ey in range(2):
        r = 8 + 16 * ey
        y = slice(16 * ey, 16 * ey + 16)
        parts = []
        for ex in range(2):
            carry = tuple((jnp.zeros((16, 128), F32),) * 2 for _ in range(3))
            for xb in range(2):
                k = (2 * ex + xb) * 4 + 2 * ey
                off = jnp.concatenate(
                    [jnp.broadcast_to(mask_s[k + h : k + h + 1, :], (8, 128)) for h in range(2)], axis=0
                )
                below, above = off < -0.5, off > 0.5

                def step(t, carry, below=below, above=above, ex=ex, xb=xb, r=r, y=y):
                    x = 16 * ex + 8 * xb + t
                    warped = jnp.where(
                        below, lo_v[x, y, :].astype(F32),
                        jnp.where(above, hi_v[x, y, :].astype(F32), own_v[x, y, :].astype(F32)),
                    )
                    misfit = fs[x + 1, r : r + 16, :] - warped
                    out = []
                    for c in range(3):
                        s1, s2 = carry[c]
                        s1 = s1 + gs[c, x, y, :] * misfit
                        out.append((s1, s2 + s1))
                    return tuple(out)

                carry = lax.fori_loop(0, 8, step, carry, unroll=4)
            parts.append([(s2 * (1.0 / 16.0), s1 - s2 * (1.0 / 16.0)) for s1, s2 in carry])
        for c in range(3):
            (a0, a1_), (b0, b1_) = parts[0][c], parts[1][c]
            rows = slice(c * 32 + 16 * ey, c * 32 + 16 * ey + 16)
            for n, value in enumerate((a0, a1_ + b0, b1_)):
                rx[n, rows, :] = value
    yr = ys[48:, :96]
    rt2[24:32, :] = jnp.zeros((8, 384), F32)
    for n in range(3):
        hi, mid, low = pieces(rx[n])
        t = mm(yr, hi) + mm(yr, mid) + mm(yr, low)
        for m in range(3):
            rt2[8 * n : 8 * n + 8, 128 * m : 128 * m + 128] = t[8 * m : 8 * m + 8]
    stacked = jnp.concatenate(pieces(rt2[...]), axis=0)
    done = mm(stacked, wr[...])
    done = done[:32] + done[32:64] + done[64:96]
    for n in range(3):
        rsend[n] = done[8 * n : 8 * n + 8]
    rcopies = []
    for n, (bx, by) in enumerate(SOURCES):
        rcopies.append(
            send(rsend, rrecv.at[bx + 2, by + 2], rsem_s.at[n], rsem_r.at[n], at(-bx, -by))
        )
    rrecv[2, 2] = rsend[...]

    lane = lax.broadcasted_iota(jnp.int32, (8, 128), 1)
    sub = lax.broadcasted_iota(jnp.int32, (8, 128), 0)
    slot, depth = lane // 16, lane % 16

    def roll(x, shift):
        shift = shift % 128
        return x if shift == 0 else pltpu.roll(x, shift, 1)

    for copy in kcopies:
        copy.wait_recv()
    in_a_diag = jnp.where(slot == 1, 1.0, jnp.where(slot == 2, ylo_ok, 0.0))
    in_b_diag = (slot >= 2) & (slot <= 4)
    for e in range(9):
        def entry(group, e=e):
            if e == 3:
                return krecv[0, group, 4] * xlo_ok + krecv[1, group, 0]
            if e == 7:
                return krecv[1, group, 4] + krecv[2, group, 0]
            if e < 3:
                return krecv[0, group, e + 1]
            if e < 7:
                return krecv[1, group, e - 3]
            return krecv[2, group, 1]

        a, b0, b1_, c = [entry(group) for group in range(4)]

        def diag(a, b, c):
            return a * in_a_diag + jnp.where(in_b_diag, b, 0.0) + jnp.where(slot == 4, c, 0.0)

        def off_diag(a, b, c):
            return jnp.where(slot < 2, a, jnp.where(slot < 4, b, jnp.where(slot == 4, c, 0.0)))

        dd = diag(roll(a, -16), b0, c)
        fd = off_diag(a, roll(b0, -48), roll(c, -16))
        df = diag(roll(a, -80), b1_, roll(c, -32))
        ff = off_diag(roll(a, -64), roll(b1_, -48), roll(c, -48))
        kf[e, 4] = dd
        kf[e, 5] = df
        kf[e, 3] = roll(df, 1)
        kf[e, 7] = fd
        kf[e, 1] = roll(fd, 16)
        kf[e, 8] = ff
        kf[e, 6] = roll(ff, 1)
        kf[e, 2] = roll(ff, 16)
        kf[e, 0] = roll(ff, 17)

    lane_j = 2 * gy + slot - 2
    lane_ok = (lane_j >= 0) & (lane_j < 64) & (slot < 6) & (depth < 9)
    lane_mask = jnp.where(lane_ok, 1.0, 0.0)
    node_mask = {i: lane_mask * flag((2 * gx + i >= 0) & (2 * gx + i < 16)) for i in range(-2, 4)}
    own_mask = jnp.where((slot >= 2) & (slot < 4) & (depth < 9), 1.0, 0.0)

    def apply(v, rows):
        need = sorted({i + ox for i in rows for ox in (-1, 0, 1)})
        first, second = {}, {}
        for i in need:
            second[i] = v[i]
            first[i] = jnp.where(sub < 3, v[i], pltpu.roll(v[i], 7, 0))
        acc1 = {i: jnp.zeros((8, 128), F32) for i in rows}
        acc2 = {i: jnp.zeros((8, 128), F32) for i in rows}
        for o in range(9):
            oy, oz = o // 3 - 1, o % 3 - 1
            s1 = {i: roll(first[i], -(16 * oy + oz)) for i in need}
            s2 = {i: roll(second[i], -(16 * oy + oz)) for i in need}
            for i in rows:
                for ox in (-1, 0, 1):
                    k = kf[2 * i + 3 + ox, o]
                    acc1[i] = acc1[i] + k * s1[i + ox]
                    acc2[i] = acc2[i] + k * s2[i + ox]
        out = {}
        for i in rows:
            total = acc1[i] + pltpu.roll(acc1[i], 5, 0)
            total = total + jnp.where(sub == 0, pltpu.roll(acc2[i], 3, 0), pltpu.roll(acc2[i], 6, 0))
            out[i] = jnp.where(sub < 3, total, jnp.where(sub < 6, pltpu.roll(total, 3, 0), pltpu.roll(total, 6, 0)))
        return out

    for copy in rcopies:
        copy.wait_recv()
    w0 = {}
    lo2_x, lo2_y = flag(gx > 1), flag(gy > 1)
    x_ok = {-2: lo2_x, -1: xlo_ok, 0: None, 1: None}
    y_ok = {-2: lo2_y, -1: ylo_ok, 0: None, 1: None}
    for i in range(-2, 4):
        total = None
        for by in (-2, -1, 0, 1):
            part = None
            for bx in (-2, -1, 0, 1):
                n = i - 2 * bx
                if 0 <= n <= 2:
                    term = rrecv[bx + 2, by + 2, n]
                    if x_ok[bx] is not None:
                        term = term * x_ok[bx]
                    part = term if part is None else part + term
            part = roll(part, 32 * by)
            if y_ok[by] is not None:
                part = part * y_ok[by]
            total = part if total is None else total + part
        w0[i] = total * node_mask[i]

    w1 = apply(w0, (-1, 0, 1, 2))
    w1 = {i: w1[i] * node_mask[i] for i in w1}
    w2_own = apply(w1, (0, 1))
    for i in range(2):
        vsend[i] = w2_own[i] * own_mask
    vcopies = []
    for n, (dx, dy) in enumerate(NEIGHBOURS):
        vcopies.append(
            send(vsend, vrecv.at[1 - dx, 1 - dy], vsem_s.at[n], vsem_r.at[n], at(dx, dy))
        )
    vrecv[1, 1] = vsend[...]

    for copy in vcopies:
        copy.wait_recv()
    w2 = {}
    for i in range(-2, 4):
        bx, n = i // 2, i % 2
        total = vrecv[bx + 1, 1, n] + roll(vrecv[bx + 1, 0, n], -32) + roll(vrecv[bx + 1, 2, n], 32)
        w2[i] = total * node_mask[i]
    w3 = apply(w2, (-1, 0, 1, 2))
    w3 = {i: w3[i] * node_mask[i] for i in w3}
    w4 = apply(w3, (0, 1))
    krylov = [w0, w1, w2, w3, w4]

    packed = [jnp.where(sub < 3, w[0], jnp.where(sub < 6, w[1], 0.0)) * own_mask for w in krylov]
    left = roll(packed[0], -32) + packed[1] + roll(packed[2], 32) + roll(packed[3], 64)
    left_halves = split(left)
    value = remainder = jnp.zeros((8, 128), F32)
    for j in range(5):
        right = packed[j] + roll(packed[j], 32)
        right = right + roll(right, 64)
        p, e = two_prod(left, left_halves, right, split(right))
        for shift in (4, 2, 1):
            p, err = two_sum(p, pltpu.roll(p, shift, 0))
            e = e + pltpu.roll(e, shift, 0) + err
        value = jnp.where(sub == j, p, value)
        remainder = jnp.where(sub == j, e, remainder)

    def pair_tree(slots):
        p, e = slots[:, 0], slots[:, 1]
        while p.shape[0] > 1:
            half = p.shape[0] // 2
            e = e[:half] + e[half:]
            p, err = two_sum(p[:half], p[half:])
            e = e + err
        return p[0], e[0]

    asrc[0] = value
    asrc[1] = remainder
    a1[gy] = asrc[...]
    for m in range(1, NGY):
        send(asrc, a1.at[gy], arsem_s.at[0], arsem_r.at[0], at(0, m))
    pltpu.make_async_copy(a1.at[pl.ds(0, NGY - 1)], a1.at[pl.ds(0, NGY - 1)], arsem_r.at[0]).wait()
    p, e = pair_tree(a1[...])
    b1src[0] = p
    b1src[1] = e
    b1[gx] = b1src[...]
    for m in range(1, NGX):
        send(b1src, b1.at[gx], arsem_s.at[1], arsem_r.at[1], at(m, 0))
    pltpu.make_async_copy(b1.at[pl.ds(0, NGX - 1)], b1.at[pl.ds(0, NGX - 1)], arsem_r.at[1]).wait()
    p, e = pair_tree(b1[...])
    for shift in (16, 8, 4, 2, 1):
        e = e + roll(e, -shift)
        p, err = two_sum(p, roll(p, -shift))
        e = e + err
    high = p + e
    low = (p - high) + e

    def few_bits(x):
        t = x * 262145.0
        return t - (t - x)

    m0, m1, m2 = high[0:1, 0:1], high[1:2, 0:1], high[1:2, 32:33]
    mean = m1 / m0
    mu = few_bits(mean)
    spread_q = few_bits(jnp.maximum(m2 / m0 - mean * mean, 1e-5 * mean * mean))
    poly = [[jnp.ones_like(m0)]]
    for k in range(4):
        new = [None] + list(poly[k])
        for i, a in enumerate(poly[k]):
            new[i] = add(new[i], -(mu * a))
        if k:
            for i, a in enumerate(poly[k - 1]):
                new[i] = new[i] - spread_q * a
        poly.append(new)

    def combine(coefficients, terms):
        total = None
        for c, (h, l) in zip(coefficients, terms):
            c = jnp.broadcast_to(c, h.shape)
            p, e = two_prod(c, split(c), h, split(h))
            e = e + c * l
            if total is None:
                total = (p, e)
            else:
                q, err = two_sum(total[0], p)
                total = (q, total[1] + e + err)
        h = total[0] + total[1]
        return h, (total[0] - h) + total[1]

    rows_w = [(high[j : j + 1], low[j : j + 1]) for j in range(5)]
    rows_q = [combine(poly[k], rows_w) for k in range(5)]
    filler = [jnp.zeros((3, 128), F32)]
    mixed = [jnp.concatenate([r[n] for r in rows_q] + filler, axis=0) for n in range(2)]
    moved = [tuple(roll(x, -32 * t) for x in mixed) for t in range(4)]
    G = {}
    for l in range(4):
        h, _ = combine(poly[l], moved)
        for k in range(l, 5):
            G[k, l] = G[l, k] = h[k : k + 1, 0:1]

    own = (0, 1)

    def times(k_of, v, older):
        return {i: k_of[i] - mu * v[i] - (0.0 if older is None else spread_q * older[i]) for i in own}

    q1 = times(w1, w0, None)
    kq1 = times(w2, w1, None)
    kkq1 = times(w3, w2, None)
    kkkq1 = times(w4, w3, None)
    q2 = times(kq1, q1, w0)
    kq2 = times(kkq1, kq1, w1)
    kkq2 = times(kkkq1, kkq1, w2)
    q3 = times(kq2, q2, q1)
    kq3 = times(kkq2, kq2, kq1)
    q4 = times(kq3, q3, q2)
    basis = [w0, q1, q2, q3, q4]

    def form(left, right):
        total = None
        for i, a in enumerate(left):
            if a is None:
                continue
            inner = None
            for j, b in enumerate(right):
                if b is None:
                    continue
                term = G[i, j] * b
                inner = term if inner is None else inner + term
            term = a * inner
            total = term if total is None else total + term
        return total

    one = jnp.ones_like(m0)
    center = mu + DAMPING
    residual = [one, None, None, None, None]
    direction = list(residual)
    update = [None] * 5
    rr = G[0, 0]
    for turn in range(ITERS):
        image = [None] * 5
        for k in range(4):
            d = direction[k]
            if d is None:
                continue
            image[k] = add(image[k], center * d)
            image[k + 1] = add(image[k + 1], d)
            if k:
                image[k - 1] = add(image[k - 1], spread_q * d)
        alpha = rr / form(direction, image)
        update = [add(u, None if d is None else alpha * d) for u, d in zip(update, direction)]
        residual = [add(r, None if q is None else -(alpha * q)) for r, q in zip(residual, image)]
        if turn < ITERS - 1:
            new = form(residual, residual)
            beta = new / rr
            direction = [add(r, None if d is None else beta * d) for r, d in zip(residual, direction)]
            rr = new
    for coords, out in ((update, upd_out), (residual, res_out)):
        for i in range(2):
            total = None
            for k in range(5):
                if coords[k] is not None:
                    term = coords[k] * basis[k][i]
                    total = term if total is None else total + term
            for j in range(2):
                moved = roll(total, -(32 + 16 * j))
                for c in range(3):
                    out[c, i, j : j + 1, :] = moved[c : c + 1, :9]

    for copy in (c_ylo, c_yhi, c_xlo, c_xhi, c_dlo, c_dhi, *kcopies, *rcopies, *vcopies):
        copy.wait_send()
    pltpu.make_async_copy(a1.at[pl.ds(0, NGY - 1)], a1.at[pl.ds(0, NGY - 1)], arsem_s.at[0]).wait()
    pltpu.make_async_copy(b1.at[pl.ds(0, NGX - 1)], b1.at[pl.ds(0, NGX - 1)], arsem_s.at[1]).wait()


def local(reference_scan, deformed_scan, source_column):
    table = source_column.reshape(NGY, 1, 64)
    consts = constants()
    vmem = pl.BlockSpec(memory_space=pltpu.VMEM)
    hbm = pl.BlockSpec(memory_space=pltpu.HBM)
    V, DMA = pltpu.VMEM, pltpu.SemaphoreType.DMA
    scratch = [
        V((1, 64), jnp.int32), V((80, 192), BF16), V((384, 128), BF16), V((128, 128), BF16), V((64, 128), BF16),
        V((32, 32, 128), BF16), V((32, 32, 128), BF16), V((32, 32, 128), BF16), V((32, 32, 128), BF16),
        V((34, 48, 128), F32), V((3, 32, 32, 128), F32), V((16, 128), F32),
        V((2, 32, 128), BF16), V((32, 128), BF16), V((32, 128), BF16), V((32, 128), BF16), V((32, 128), BF16),
        V((5, 192, 128), F32), V((48, 640), F32), V((4, 5, 8, 128), F32), V((3, 4, 5, 8, 128), F32),
        V((3, 96, 128), F32), V((32, 384), F32), V((3, 8, 128), F32), V((4, 4, 3, 8, 128), F32),
        V((9, 9, 8, 128), F32), V((640, 512), BF16), V((2, 8, 128), F32), V((3, 3, 2, 8, 128), F32),
        V((2, 8, 128), F32), V((NGY, 2, 8, 128), F32), V((2, 8, 128), F32), V((NGX, 2, 8, 128), F32),
        DMA((8,)), DMA((6,)), DMA((6,)), DMA((8,)), DMA((8,)), DMA((15,)), DMA((15,)), DMA((8,)), DMA((8,)),
        DMA((2,)), DMA((2,)),
    ]
    out = jax.ShapeDtypeStruct((3, 2, 2, 9), F32)
    return pl.pallas_call(
        kernel,
        out_shape=(out, out),
        in_specs=[hbm] * 8,
        out_specs=(vmem, vmem),
        scratch_shapes=scratch,
        compiler_params=pltpu.CompilerParams(
            collective_id=0, has_side_effects=True, vmem_limit_bytes=55210 * 1024
        ),
    )(reference_scan, deformed_scan, table, *consts)


def solution(mesh):
    return jax.shard_map(
        local,
        mesh=mesh,
        in_specs=(P("gx", "gy", None), P("gx", "gy", None), P("gx", None, None, None)),
        out_specs=(P(None, "gx", "gy", None), P(None, "gx", "gy", None)),
        check_vma=False,
    )
```

```python
import functools

import jax
import jax.numpy as jnp
import ml_dtypes
import numpy as np
from jax import lax
from jax.experimental import pallas as pl
from jax.experimental.pallas import tpu as pltpu
from jax.sharding import PartitionSpec as P

MESH = pl.DeviceIdType.MESH
E = 16
ITERS = 4
DAMPING = 0.1
NGX, NGY = 8, 32
F32, BF16 = jnp.float32, jnp.bfloat16

NEIGHBOURS = [(dx, dy) for dx in (-1, 0, 1) for dy in (-1, 0, 1) if (dx, dy) != (0, 0)]
SOURCES = [(bx, by) for bx in (-2, -1, 0, 1) for by in (-2, -1, 0, 1) if (bx, by) != (0, 0)]
SOURCES.sort(key=lambda b: -abs(b[0]) - 0.9 * abs(b[1]))
NEIGHBOURS.sort(key=lambda b: -abs(b[0]) - abs(b[1]))
FAR_Y = sorted(range(1, NGY), key=lambda m: -min(m // 8, 4 - m // 8) - min(m % 8, 8 - m % 8) / 2)
FAR_X = sorted(range(1, NGX), key=lambda m: -min(m, NGX - m))
PAIRS = [(0, 0), (1, 1), (2, 2), (0, 1), (1, 2), (2, 0)]


def hat(position):
    return np.maximum(0.0, 1.0 - np.abs(position) / E)


def chain(count, nodes):
    position = np.arange(count)
    w = np.stack([hat(position - E * n) for n in range(nodes)])
    out = []
    for n in range(nodes):
        out.append(w[n] * w[n])
        if n + 1 < nodes:
            out.append(w[n] * w[n + 1])
    return w, np.stack(out)


def constants():
    wy, cy = chain(32, 3)
    wz, cz = chain(128, 9)
    scale = 1.0 / 1024.0
    ymat = np.zeros((48, 192))
    for m in range(5):
        for p in range(6):
            ymat[m * 8 + p, p * 32 : (p + 1) * 32] = cy[m] * scale
    zd, zf = np.zeros((128, 16)), np.zeros((128, 16))
    zd[:, :9] = cz[0::2].T
    zf[:, :8] = cz[1::2].T
    wmat = np.zeros((5, 128, 4, 8, 16))
    D0, F0, D1, F1, D2 = range(5)
    place = {
        (0, 0): (F0, zd), (0, 1): (F1, zd), (0, 2): (D1, zd), (0, 3): (D2, zd),
        (0, 4): (F0, zf), (0, 5): (F1, zf), (0, 6): (D1, zf), (0, 7): (D2, zf),
        (1, 2): (D0, zd), (1, 3): (D1, zd), (1, 4): (D2, zd), (1, 5): (F0, zd), (1, 6): (F1, zd),
        (2, 2): (D0, zf), (2, 3): (D1, zf), (2, 4): (D2, zf), (2, 5): (F0, zf), (2, 6): (F1, zf),
        (3, 4): (D0, zd), (3, 5): (F0, zd), (3, 6): (D0, zf), (3, 7): (F0, zf),
    }
    for (group, block), (m, z) in place.items():
        wmat[m, :, group, block, :] = z
    wmat = wmat.reshape(640, 512)
    yr = np.zeros((32, 96))
    for n in range(3):
        for r in range(8):
            c = r % 3
            yr[n * 8 + r, c * 32 : (c + 1) * 32] = wy[n] / 32.0
    wr = np.zeros((3, 128, 8, 16))
    for n in range(3):
        wr[n, :, n, :9] = wr[n, :, 4 + n, :9] = wz.T
    wr = wr.reshape(384, 128)
    dz = np.zeros((128, 128))
    for z in range(128):
        if z + 1 < 128:
            dz[z + 1, z] = 1.0
        if z > 0:
            dz[z - 1, z] = -1.0
    lanes = np.arange(128)
    spread = (np.arange(64)[:, None] % 4 == lanes[None, :] // 32).astype(np.float64)
    cast = lambda a: a.astype(ml_dtypes.bfloat16)
    both = np.zeros((80, 192))
    both[:48] = ymat
    both[48:, :96] = yr
    return [cast(a) for a in (both, wmat, wr, dz, spread)]


def pieces(x):
    hi = x.astype(BF16)
    rest = x - hi.astype(F32)
    mid = rest.astype(BF16)
    low = (rest - mid.astype(F32)).astype(BF16)
    return hi, mid, low


def two_sum(a, b):
    s = a + b
    t = s - a
    return s, (a - (s - t)) + (b - t)


def split(a):
    t = a * 4097.0
    high = t - (t - a)
    return high, a - high


def two_prod(a, a_halves, b, b_halves):
    p = a * b
    (ah, al), (bh, bl) = a_halves, b_halves
    return p, ((ah * bh - p) + ah * bl + al * bh) + al * bl


def add(a, b):
    return b if a is None else (a if b is None else a + b)


def mm(a, b):
    return jnp.dot(a, b, preferred_element_type=F32)


def kernel(
    ref_h, def_h, table_h, ys_h, wmat_h, wr_h, dz_h, spread_h,
    upd_out, res_out,
    table, ys, wr, dz, spread,
    ref_v, own_v, def_v, fs, gs, mask_s, yface, faces,
    xs, t2, ksend, krecv, rx, rt2, rsend, rrecv, kf, wmat, vsend, vrecv,
    asrc, a1, b1src, b1,
    ktotal, lsem, sems,
):
    gx, gy = lax.axis_index("gx"), lax.axis_index("gy")

    gx_at = [lax.rem(gx + d, NGX) for d in range(NGX)]
    gy_at = [lax.rem(gy + d, NGY) for d in range(NGY)]

    def at(dx, dy):
        return (gx_at[dx % NGX], gy_at[dy % NGY])

    load_ref = pltpu.make_async_copy(ref_h, ref_v, lsem.at[0])
    load_own = pltpu.make_async_copy(def_h, own_v, lsem.at[1])
    load_w = pltpu.make_async_copy(wmat_h, wmat, lsem.at[2])
    small = [(table_h.at[gy], table), (spread_h, spread), (dz_h, dz), (ys_h, ys), (wr_h, wr)]
    small = [pltpu.make_async_copy(src, dst, lsem.at[3 + n]) for n, (src, dst) in enumerate(small)]
    load_ref.start()

    barrier = pltpu.get_barrier_semaphore()
    partners = [at(0, 1), at(0, -1), at(1, 0), at(-1, 0)]
    partners += [at(bx, by) for bx, by in SOURCES if bx != 0 and by != 0]
    partners += [at(0, m) for m in range(2, NGY - 1)] + [at(m, 0) for m in range(2, NGX - 1)]
    for partner in partners:
        pl.semaphore_signal(barrier, inc=1, device_id=partner, device_id_type=MESH)
    for copy in (*small, load_own, load_w):
        copy.start()

    def flag(condition):
        return jnp.where(condition, 1.0, 0.0).astype(F32)

    xlo_ok, xhi_ok = flag(gx > 0), flag(gx < NGX - 1)
    ylo_ok, yhi_ok = flag(gy > 0), flag(gy < NGY - 1)

    load_ref.wait()
    yface[0] = jnp.concatenate([ref_v[x, 24:32, :].astype(F32)[7:8] for x in range(32)], axis=0).astype(BF16)
    yface[1] = jnp.concatenate([ref_v[x, 0:8, :].astype(F32)[0:1] for x in range(32)], axis=0).astype(BF16)

    pl.semaphore_wait(barrier, len(partners))

    def send(src, dst, s, r, to):
        pltpu.make_async_remote_copy(
            src_ref=src, dst_ref=dst, send_sem=s, recv_sem=r, device_id=to, device_id_type=MESH
        ).start()

    def wait(as_much, sem):
        pltpu.make_async_copy(as_much, as_much, sem).wait()

    send(yface.at[0], faces.at[0], sems.at[0, 0], sems.at[0, 1], at(0, 1))
    send(yface.at[1], faces.at[1], sems.at[0, 0], sems.at[0, 1], at(0, -1))
    send(ref_h.at[31], faces.at[2], sems.at[0, 0], sems.at[0, 1], at(1, 0))
    send(ref_h.at[0], faces.at[3], sems.at[0, 0], sems.at[0, 1], at(-1, 0))
    send(def_h, def_v.at[0], sems.at[1, 0], sems.at[1, 1], at(0, 1))
    send(def_h, def_v.at[1], sems.at[1, 0], sems.at[1, 1], at(0, -1))
    for copy in small:
        copy.wait()
    row = (table[...] - gy).astype(F32)
    r16 = lax.broadcasted_iota(jnp.int32, (16, 64), 0)
    c64 = lax.broadcasted_iota(jnp.int32, (16, 64), 1)
    picked = jnp.where(c64 // 4 == r16, jnp.broadcast_to(row, (16, 64)), 0.0).astype(BF16)
    mask_s[...] = mm(picked, spread[...])

    for x in range(32):
        plane = ref_v[x]
        fs[x + 1, 8:40, :] = plane.astype(F32)
        gs[2, x] = mm(plane, dz[...])
    wait(faces, sems.at[0, 1])
    fs[0, 8:40, :] = faces[2].astype(F32) * xlo_ok
    fs[33, 8:40, :] = faces[3].astype(F32) * xhi_ok
    face_lo = faces[0].astype(F32) * ylo_ok
    face_hi = faces[1].astype(F32) * yhi_ok
    for x in range(32):
        fs[x + 1, 7:8, :] = face_lo[x : x + 1]
        fs[x + 1, 40:41, :] = face_hi[x : x + 1]

    for ey in range(2):
        r = 8 + 16 * ey
        y = slice(16 * ey, 16 * ey + 16)
        moments = []
        for ex in range(2):
            def step(t, carry, ex=ex, r=r, y=y):
                x = 16 * ex + t
                g = (
                    fs[x + 2, r : r + 16, :] - fs[x, r : r + 16, :],
                    fs[x + 1, r + 1 : r + 17, :] - fs[x + 1, r - 1 : r + 15, :],
                    gs[2, x, y, :],
                )
                gs[0, x, y, :] = g[0]
                gs[1, x, y, :] = g[1]
                out = []
                for p, (c, d) in enumerate(PAIRS):
                    s1, s2, s3 = carry[p]
                    s1 = s1 + g[c] * g[d]
                    s2 = s2 + s1
                    s3 = s3 + s2
                    out.append((s1, s2, s3))
                return tuple(out)

            zero = jnp.zeros((16, 128), F32)
            sums = lax.fori_loop(0, 16, step, tuple((zero,) * 3 for _ in PAIRS), unroll=4)
            weighted = []
            for s1, s2, s3 in sums:
                m00 = (2.0 * s3 - s2) * (1.0 / 256.0)
                first = s2 * (1.0 / 16.0)
                weighted.append((m00, first - m00, s1 - 2.0 * first + m00))
            moments.append(weighted)
        for p in range(6):
            (a00, a01, a11), (b00, b01, b11) = moments[0][p], moments[1][p]
            rows = slice(p * 32 + 16 * ey, p * 32 + 16 * ey + 16)
            for u, value in enumerate((a00, a01, a11 + b00, b01, b11)):
                xs[u, rows, :] = value

    lane = lax.broadcasted_iota(jnp.int32, (8, 128), 1)
    sub = lax.broadcasted_iota(jnp.int32, (8, 128), 0)

    load_own.wait()
    wait(def_v, sems.at[1, 1])
    for ey in range(2):
        r = 8 + 16 * ey
        y = slice(16 * ey, 16 * ey + 16)
        parts = []
        for ex in range(2):
            carry = tuple((jnp.zeros((16, 128), F32),) * 2 for _ in range(3))
            for xb in range(2):
                k = (2 * ex + xb) * 4 + 2 * ey
                off = jnp.concatenate(
                    [jnp.broadcast_to(mask_s[k + h : k + h + 1, :], (8, 128)) for h in range(2)], axis=0
                )
                below, above = off < -0.5, off > 0.5

                def step(t, carry, below=below, above=above, ex=ex, xb=xb, r=r, y=y):
                    x = 16 * ex + 8 * xb + t
                    warped = jnp.where(
                        below, def_v[0, x, y, :].astype(F32),
                        jnp.where(above, def_v[1, x, y, :].astype(F32), own_v[x, y, :].astype(F32)),
                    )
                    misfit = fs[x + 1, r : r + 16, :] - warped
                    out = []
                    for c in range(3):
                        s1, s2 = carry[c]
                        s1 = s1 + gs[c, x, y, :] * misfit
                        out.append((s1, s2 + s1))
                    return tuple(out)

                carry = lax.fori_loop(0, 8, step, carry, unroll=4)
            parts.append([(s2 * (1.0 / 16.0), s1 - s2 * (1.0 / 16.0)) for s1, s2 in carry])
        for c in range(3):
            (a0, a1_), (b0, b1_) = parts[0][c], parts[1][c]
            rows = slice(c * 32 + 16 * ey, c * 32 + 16 * ey + 16)
            for n, value in enumerate((a0, a1_ + b0, b1_)):
                rx[n, rows, :] = value
    yr = ys[48:, :96]
    rt2[24:32, :] = jnp.zeros((8, 384), F32)
    for n in range(3):
        hi, mid, low = pieces(rx[n])
        t = mm(yr, hi) + mm(yr, mid) + mm(yr, low)
        for m in range(3):
            rt2[8 * n : 8 * n + 8, 128 * m : 128 * m + 128] = t[8 * m : 8 * m + 8]
    stacked = jnp.concatenate(pieces(rt2[...]), axis=0)
    done = mm(stacked, wr[...])
    done = done[:32] + done[32:64] + done[64:96]
    rsend[...] = jnp.where(lane < 64, jnp.where(sub < 3, done[:8], done[8:16]), done[16:24])
    for bx, by in SOURCES:
        send(rsend, rrecv.at[4 * bx + by + 10], sems.at[3, 0], sems.at[3, 1], at(-bx, -by))
    rrecv[10] = rsend[...]

    ymat = ys[:48, :]
    t2[40:48, :] = jnp.zeros((8, 640), F32)
    for u in range(5):
        hi, mid, low = pieces(xs[u])
        t = mm(ymat, hi) + mm(ymat, mid) + mm(ymat, low)
        for m in range(5):
            t2[8 * u : 8 * u + 8, 128 * m : 128 * m + 128] = t[8 * m : 8 * m + 8]
    load_w.wait()
    stacked = jnp.concatenate(pieces(t2[...]), axis=0)
    done = mm(stacked, wmat[...])
    done = done[:48] + done[48:96] + done[96:144]
    for u in range(5):
        for group in range(4):
            ksend[group, u] = done[8 * u : 8 * u + 8, 128 * group : 128 * group + 128]

    GROUP = {1: (0, 1), 0: (1, 2), -1: (3, 1)}
    UNIT = {1: (1, 4), 0: (0, 5), -1: (0, 2)}
    for dx, dy in NEIGHBOURS:
        g0, gn = GROUP[dy]
        u0, un = UNIT[dx]
        send(
            ksend.at[pl.ds(g0, gn), pl.ds(u0, un)],
            krecv.at[1 - dx, pl.ds(g0, gn), pl.ds(u0, un)],
            sems.at[2, 0], sems.at[2, 1], at(dx, dy),
        )
    krecv[1, 1:3] = ksend[1:3]

    slot, depth = lane // 16, lane % 16

    def roll(x, shift):
        shift = shift % 128
        return x if shift == 0 else pltpu.roll(x, shift, 1)

    wait(ktotal, sems.at[2, 1])
    in_a_diag = jnp.where(slot == 1, 1.0, jnp.where(slot == 2, ylo_ok, 0.0))
    in_b_diag = (slot >= 2) & (slot <= 4)
    for e in range(9):
        def entry(group, e=e):
            if e == 3:
                return krecv[0, group, 4] * xlo_ok + krecv[1, group, 0]
            if e == 7:
                return krecv[1, group, 4] + krecv[2, group, 0]
            if e < 3:
                return krecv[0, group, e + 1]
            if e < 7:
                return krecv[1, group, e - 3]
            return krecv[2, group, 1]

        a, b0, b1_, c = [entry(group) for group in range(4)]

        def diag(a, b, c):
            return a * in_a_diag + jnp.where(in_b_diag, b, 0.0) + jnp.where(slot == 4, c, 0.0)

        def off_diag(a, b, c):
            return jnp.where(slot < 2, a, jnp.where(slot < 4, b, jnp.where(slot == 4, c, 0.0)))

        dd = diag(roll(a, -16), b0, c)
        fd = off_diag(a, roll(b0, -48), roll(c, -16))
        df = diag(roll(a, -80), b1_, roll(c, -32))
        ff = off_diag(roll(a, -64), roll(b1_, -48), roll(c, -48))
        kf[e, 4] = dd
        kf[e, 5] = df
        kf[e, 3] = roll(df, 1)
        kf[e, 7] = fd
        kf[e, 1] = roll(fd, 16)
        kf[e, 8] = ff
        kf[e, 6] = roll(ff, 1)
        kf[e, 2] = roll(ff, 16)
        kf[e, 0] = roll(ff, 17)

    lane_j = 2 * gy + slot - 2
    lane_ok = (lane_j >= 0) & (lane_j < 64) & (slot < 6) & (depth < 9)
    lane_mask = jnp.where(lane_ok, 1.0, 0.0)
    node_mask = {i: lane_mask * flag((2 * gx + i >= 0) & (2 * gx + i < 16)) for i in range(-2, 4)}
    own_mask = jnp.where((slot >= 2) & (slot < 4) & (depth < 9), 1.0, 0.0)

    def apply(v, rows):
        need = sorted({i + ox for i in rows for ox in (-1, 0, 1)})
        first, second = {}, {}
        for i in need:
            second[i] = v[i]
            first[i] = jnp.where(sub < 3, v[i], pltpu.roll(v[i], 7, 0))
        acc1 = {i: jnp.zeros((8, 128), F32) for i in rows}
        acc2 = {i: jnp.zeros((8, 128), F32) for i in rows}
        for o in range(9):
            oy, oz = o // 3 - 1, o % 3 - 1
            s1 = {i: roll(first[i], -(16 * oy + oz)) for i in need}
            s2 = {i: roll(second[i], -(16 * oy + oz)) for i in need}
            for i in rows:
                for ox in (-1, 0, 1):
                    k = kf[2 * i + 3 + ox, o]
                    acc1[i] = acc1[i] + k * s1[i + ox]
                    acc2[i] = acc2[i] + k * s2[i + ox]
        out = {}
        for i in rows:
            total = acc1[i] + pltpu.roll(acc1[i], 5, 0)
            total = total + jnp.where(sub == 0, pltpu.roll(acc2[i], 3, 0), pltpu.roll(acc2[i], 6, 0))
            out[i] = jnp.where(sub < 3, total, jnp.where(sub < 6, pltpu.roll(total, 3, 0), pltpu.roll(total, 6, 0)))
        return out

    wait(rrecv.at[pl.ds(0, 15)], sems.at[3, 1])
    w0 = {}
    lo2_x, lo2_y = flag(gx > 1), flag(gy > 1)
    x_ok = {-2: lo2_x, -1: xlo_ok, 0: None, 1: None}
    y_ok = {-2: lo2_y, -1: ylo_ok, 0: None, 1: None}
    totals = {i: None for i in range(-2, 4)}
    for by in (-2, -1, 0, 1):
        part = {i: None for i in range(-2, 4)}
        for bx in (-2, -1, 0, 1):
            tile = rrecv[4 * bx + by + 10]
            if x_ok[bx] is not None:
                tile = tile * x_ok[bx]
            for n in range(3):
                i = 2 * bx + n
                if i in part:
                    shifted = (tile, pltpu.roll(tile, 5, 0), roll(tile, 64))[n]
                    part[i] = add(part[i], shifted)
        for i in part:
            here = jnp.where(lane < 48, part[i], 0.0)
            if y_ok[by] is not None:
                here = here * y_ok[by]
            totals[i] = add(totals[i], roll(here, 32 * (by + 1)))
    for i in totals:
        t = totals[i]
        t = jnp.where(sub < 3, t, jnp.where(sub < 6, pltpu.roll(t, 3, 0), pltpu.roll(t, 6, 0)))
        w0[i] = t * node_mask[i]

    w1 = apply(w0, (-1, 0, 1, 2))
    w1 = {i: w1[i] * node_mask[i] for i in w1}
    w2_own = apply(w1, (0, 1))
    vsend[...] = jnp.where(sub < 3, w2_own[0], w2_own[1]) * own_mask
    for dx, dy in NEIGHBOURS:
        send(vsend, vrecv.at[4 - 3 * dx - dy], sems.at[4, 0], sems.at[4, 1], at(dx, dy))
    vrecv[4] = vsend[...]

    wait(vrecv.at[pl.ds(0, 8)], sems.at[4, 1])
    w2 = {}
    for i in range(-2, 4):
        if i % 2 == 0:
            b = 3 * (i // 2) + 4
            t = vrecv[b] + roll(vrecv[b - 1], -32) + roll(vrecv[b + 1], 32)
            back, ahead = pltpu.roll(t, 5, 0), pltpu.roll(t, 3, 0)
            total = jnp.where(sub < 3, t, jnp.where(sub < 6, ahead, pltpu.roll(t, 6, 0)))
        else:
            total = jnp.where(sub < 3, back, jnp.where(sub < 6, t, ahead))
        w2[i] = total * node_mask[i]
    w3 = apply(w2, (-1, 0, 1, 2))
    w3 = {i: w3[i] * node_mask[i] for i in w3}
    w4 = apply(w3, (0, 1))
    krylov = [w0, w1, w2, w3, w4]

    packed = [jnp.where(sub < 3, w[0], jnp.where(sub < 6, w[1], 0.0)) * own_mask for w in krylov]
    left = roll(packed[0], -32) + packed[1] + roll(packed[2], 32) + roll(packed[3], 64)
    left_halves = split(left)
    value = remainder = jnp.zeros((8, 128), F32)
    for j in range(5):
        right = packed[j] + roll(packed[j], 32)
        right = right + roll(right, 64)
        p, e = two_prod(left, left_halves, right, split(right))
        for shift in (4, 2, 1):
            p, err = two_sum(p, pltpu.roll(p, shift, 0))
            e = e + pltpu.roll(e, shift, 0) + err
        value = jnp.where(sub == j, p, value)
        remainder = jnp.where(sub == j, e, remainder)

    for shift in (16, 8, 4, 2, 1):
        remainder = remainder + roll(remainder, -shift)
        value, err = two_sum(value, roll(value, -shift))
        remainder = remainder + err
    line = jnp.zeros((1, 128), F32)
    first = (lane % 32 == 0)[:1]
    for j in range(5):
        line = line + roll(jnp.where(first, value[j : j + 1], 0.0), j)
        line = line + roll(jnp.where(first, remainder[j : j + 1], 0.0), 8 + j)

    def line_tree(slots):
        p, e = slots, None
        while p.shape[0] > 1:
            half = p.shape[0] // 2
            p, err = two_sum(p[:half], p[half:])
            e = err if e is None else e[:half] + e[half:] + err
        return p[0], e[0]

    asrc[...] = line
    a1[gy] = line
    for m in FAR_Y:
        send(asrc, a1.at[gy], sems.at[5, 0], sems.at[5, 1], at(0, m))
    wait(a1.at[pl.ds(0, NGY - 1)], sems.at[5, 1])
    p, e = line_tree(a1[...])
    line = jnp.where((lane % 16 < 8)[:1], p, p + roll(e, 8))
    b1src[...] = line
    b1[gx] = line
    for m in FAR_X:
        send(b1src, b1.at[gx], sems.at[6, 0], sems.at[6, 1], at(m, 0))
    wait(b1.at[pl.ds(0, NGX - 1)], sems.at[6, 1])
    p, e = line_tree(b1[...])
    e = e + roll(p, -8)
    high = p + e
    low = (p - high) + e

    def few_bits(x):
        t = x * 262145.0
        return t - (t - x)

    m0, m1, m2 = [jnp.broadcast_to(high[:, n : n + 1], (8, 128)) for n in (0, 1, 33)]
    mean = m1 / m0
    mu = few_bits(mean)
    spread_q = few_bits(jnp.maximum(m2 / m0 - mean * mean, 1e-5 * mean * mean))
    poly = [[jnp.ones_like(m0)]]
    for k in range(4):
        new = [None] + list(poly[k])
        for i, a in enumerate(poly[k]):
            new[i] = add(new[i], -(mu * a))
        if k:
            for i, a in enumerate(poly[k - 1]):
                new[i] = new[i] - spread_q * a
        poly.append(new)

    def combine(coefficients, terms):
        total = None
        for c, (h, l) in zip(coefficients, terms):
            c = c[: h.shape[0]]
            p, e = two_prod(c, split(c), h, split(h))
            e = e + c * l
            if total is None:
                total = (p, e)
            else:
                q, err = two_sum(total[0], p)
                total = (q, total[1] + e + err)
        h = total[0] + total[1]
        return h, (total[0] - h) + total[1]

    rows_w = [(roll(high, -j), roll(low, -j)) for j in range(5)]
    rows_q = [combine(poly[k], rows_w) for k in range(5)]
    filler = [jnp.zeros((3, 128), F32)]
    mixed = [jnp.concatenate([r[n] for r in rows_q] + filler, axis=0) for n in range(2)]
    moved = [tuple(roll(x, -32 * t) for x in mixed) for t in range(4)]
    G = {}
    for l in range(4):
        h, _ = combine(poly[l], moved)
        for k in range(l, 5):
            G[k, l] = G[l, k] = jnp.broadcast_to(h[k : k + 1, 0:1], (8, 128))

    own = (0, 1)

    def times(k_of, v, older):
        return {i: k_of[i] - mu * v[i] - (0.0 if older is None else spread_q * older[i]) for i in own}

    q1 = times(w1, w0, None)
    kq1 = times(w2, w1, None)
    kkq1 = times(w3, w2, None)
    kkkq1 = times(w4, w3, None)
    q2 = times(kq1, q1, w0)
    kq2 = times(kkq1, kq1, w1)
    kkq2 = times(kkkq1, kkq1, w2)
    q3 = times(kq2, q2, q1)
    kq3 = times(kkq2, kq2, kq1)
    q4 = times(kq3, q3, q2)
    basis = [w0, q1, q2, q3, q4]

    def form(left, right):
        total = None
        for i, a in enumerate(left):
            if a is None:
                continue
            inner = None
            for j, b in enumerate(right):
                if b is None:
                    continue
                term = G[i, j] * b
                inner = term if inner is None else inner + term
            term = a * inner
            total = term if total is None else total + term
        return total

    one = jnp.ones_like(m0)
    center = mu + DAMPING
    residual = [one, None, None, None, None]
    direction = list(residual)
    update = [None] * 5
    rr = G[0, 0]
    for turn in range(ITERS):
        image = [None] * 5
        for k in range(4):
            d = direction[k]
            if d is None:
                continue
            image[k] = add(image[k], center * d)
            image[k + 1] = add(image[k + 1], d)
            if k:
                image[k - 1] = add(image[k - 1], spread_q * d)
        alpha = rr / form(direction, image)
        update = [add(u, None if d is None else alpha * d) for u, d in zip(update, direction)]
        residual = [add(r, None if q is None else -(alpha * q)) for r, q in zip(residual, image)]
        if turn < ITERS - 1:
            new = form(residual, residual)
            beta = new / rr
            direction = [add(r, None if d is None else beta * d) for r, d in zip(residual, direction)]
            rr = new
    for coords, out in ((update, upd_out), (residual, res_out)):
        for i in range(2):
            total = None
            for k in range(5):
                if coords[k] is not None:
                    term = coords[k] * basis[k][i]
                    total = term if total is None else total + term
            for j in range(2):
                moved = roll(total, -(32 + 16 * j))
                for c in range(3):
                    out[c, i, j : j + 1, :] = moved[c : c + 1, :9]

    sent = (faces, def_v, ktotal, rrecv.at[pl.ds(0, 15)], vrecv.at[pl.ds(0, 8)], a1.at[pl.ds(0, NGY - 1)], b1.at[pl.ds(0, NGX - 1)])
    for n, as_much in enumerate(sent):
        wait(as_much, sems.at[n, 0])


def local(reference_scan, deformed_scan, source_column):
    table = source_column.reshape(NGY, 1, 64)
    consts = constants()
    vmem = pl.BlockSpec(memory_space=pltpu.VMEM)
    hbm = pl.BlockSpec(memory_space=pltpu.HBM)
    V, DMA = pltpu.VMEM, pltpu.SemaphoreType.DMA
    scratch = [
        V((1, 64), jnp.int32), V((80, 192), BF16), V((384, 128), BF16), V((128, 128), BF16), V((64, 128), BF16),
        V((32, 32, 128), BF16), V((32, 32, 128), BF16), V((2, 32, 32, 128), BF16),
        V((34, 48, 128), F32), V((3, 32, 32, 128), F32), V((16, 128), F32),
        V((2, 32, 128), BF16), V((4, 32, 128), BF16),
        V((5, 192, 128), F32), V((48, 640), F32), V((4, 5, 8, 128), F32), V((3, 4, 5, 8, 128), F32),
        V((3, 96, 128), F32), V((32, 384), F32), V((8, 128), F32), V((16, 8, 128), F32),
        V((9, 9, 8, 128), F32), V((640, 512), BF16), V((8, 128), F32), V((9, 8, 128), F32),
        V((1, 128), F32), V((NGY, 1, 128), F32), V((1, 128), F32), V((NGX, 1, 128), F32),
        V((34, 8, 128), F32), DMA((8,)), DMA((7, 2)),
    ]
    out = jax.ShapeDtypeStruct((3, 2, 2, 9), F32)
    return pl.pallas_call(
        kernel,
        out_shape=(out, out),
        in_specs=[hbm] * 8,
        out_specs=(vmem, vmem),
        scratch_shapes=scratch,
        compiler_params=pltpu.CompilerParams(
            collective_id=0, has_side_effects=True, vmem_limit_bytes=55210 * 1024
        ),
    )(reference_scan, deformed_scan, table, *consts)


def solution(mesh):
    return jax.shard_map(
        local,
        mesh=mesh,
        in_specs=(P("gx", "gy", None), P("gx", "gy", None), P("gx", None, None, None)),
        out_specs=(P(None, "gx", "gy", None), P(None, "gx", "gy", None)),
        check_vma=False,
    )
```

```python
import functools

import jax
import jax.numpy as jnp
import ml_dtypes
import numpy as np
from jax import lax
from jax.experimental import pallas as pl
from jax.experimental.pallas import tpu as pltpu
from jax.sharding import PartitionSpec as P

MESH = pl.DeviceIdType.MESH
E = 16
ITERS = 4
DAMPING = 0.1
NGX, NGY = 8, 32
F32, BF16 = jnp.float32, jnp.bfloat16

NEIGHBOURS = [(dx, dy) for dx in (-1, 0, 1) for dy in (-1, 0, 1) if (dx, dy) != (0, 0)]
SOURCES = [(bx, by) for bx in (-2, -1, 0, 1) for by in (-2, -1, 0, 1) if (bx, by) != (0, 0)]
SOURCES.sort(key=lambda b: -abs(b[0]) - 0.9 * abs(b[1]))
NEIGHBOURS.sort(key=lambda b: -abs(b[0]) - abs(b[1]))
FAR_Y = sorted(range(1, NGY), key=lambda m: -min(m // 8, 4 - m // 8) - min(m % 8, 8 - m % 8) / 2)
FAR_X = sorted(range(1, NGX), key=lambda m: -min(m, NGX - m))
PAIRS = [(0, 0), (1, 1), (2, 2), (0, 1), (1, 2), (2, 0)]


def hat(position):
    return np.maximum(0.0, 1.0 - np.abs(position) / E)


def chain(count, nodes):
    position = np.arange(count)
    w = np.stack([hat(position - E * n) for n in range(nodes)])
    out = []
    for n in range(nodes):
        out.append(w[n] * w[n])
        if n + 1 < nodes:
            out.append(w[n] * w[n + 1])
    return w, np.stack(out)


def constants():
    wy, cy = chain(32, 3)
    wz, cz = chain(128, 9)
    scale = 1.0 / 1024.0
    ymat = np.zeros((48, 192))
    for m in range(5):
        for p in range(6):
            ymat[m * 8 + p, p * 32 : (p + 1) * 32] = cy[m] * scale
    zd, zf = np.zeros((128, 16)), np.zeros((128, 16))
    zd[:, :9] = cz[0::2].T
    zf[:, :8] = cz[1::2].T
    wmat = np.zeros((5, 128, 4, 8, 16))
    D0, F0, D1, F1, D2 = range(5)
    place = {
        (0, 0): (F0, zd), (0, 1): (F1, zd), (0, 2): (D1, zd), (0, 3): (D2, zd),
        (0, 4): (F0, zf), (0, 5): (F1, zf), (0, 6): (D1, zf), (0, 7): (D2, zf),
        (1, 2): (D0, zd), (1, 3): (D1, zd), (1, 4): (D2, zd), (1, 5): (F0, zd), (1, 6): (F1, zd),
        (2, 2): (D0, zf), (2, 3): (D1, zf), (2, 4): (D2, zf), (2, 5): (F0, zf), (2, 6): (F1, zf),
        (3, 4): (D0, zd), (3, 5): (F0, zd), (3, 6): (D0, zf), (3, 7): (F0, zf),
    }
    for (group, block), (m, z) in place.items():
        wmat[m, :, group, block, :] = z
    wmat = wmat.reshape(640, 512)
    yr = np.zeros((32, 96))
    for n in range(3):
        for r in range(8):
            c = r % 3
            yr[n * 8 + r, c * 32 : (c + 1) * 32] = wy[n] / 32.0
    wr = np.zeros((3, 128, 8, 16))
    for n in range(3):
        wr[n, :, n, :9] = wr[n, :, 4 + n, :9] = wz.T
    wr = wr.reshape(384, 128)
    dz = np.zeros((128, 128))
    for z in range(128):
        if z + 1 < 128:
            dz[z + 1, z] = 1.0
        if z > 0:
            dz[z - 1, z] = -1.0
    lanes = np.arange(128)
    spread = (np.arange(64)[:, None] % 4 == lanes[None, :] // 32).astype(np.float64)
    cast = lambda a: a.astype(ml_dtypes.bfloat16)
    both = np.zeros((80, 192))
    both[:48] = ymat
    both[48:, :96] = yr
    return [cast(a) for a in (both, wmat, wr, dz, spread)]


def pieces(x):
    hi = x.astype(BF16)
    rest = x - hi.astype(F32)
    mid = rest.astype(BF16)
    low = (rest - mid.astype(F32)).astype(BF16)
    return hi, mid, low


def two_sum(a, b):
    s = a + b
    t = s - a
    return s, (a - (s - t)) + (b - t)


def split(a):
    t = a * 4097.0
    high = t - (t - a)
    return high, a - high


def two_prod(a, a_halves, b, b_halves):
    p = a * b
    (ah, al), (bh, bl) = a_halves, b_halves
    return p, ((ah * bh - p) + ah * bl + al * bh) + al * bl


def add(a, b):
    return b if a is None else (a if b is None else a + b)


def mm(a, b):
    return jnp.dot(a, b, preferred_element_type=F32)


def kernel(
    ref_h, def_h, table_h, ys_h, wmat_h, wr_h, dz_h, spread_h,
    out_ref,
    table, ys, wr, dz, spread,
    ref_v, own_v, def_v, fs, gs, mask_s, yface, faces,
    xs, t2, ksend, krecv, rx, rt2, rsend, rrecv, kf, wmat, vsend, vrecv,
    asrc, a1, b1src, b1,
    ktotal, lsem, sems,
):
    gx, gy = lax.axis_index("gx"), lax.axis_index("gy")

    gx_at = [lax.rem(gx + d, NGX) for d in range(NGX)]
    gy_at = [lax.rem(gy + d, NGY) for d in range(NGY)]

    def at(dx, dy):
        return (gx_at[dx % NGX], gy_at[dy % NGY])

    load_ref = pltpu.make_async_copy(ref_h, ref_v, lsem.at[0])
    load_own = pltpu.make_async_copy(def_h, own_v, lsem.at[1])
    load_w = pltpu.make_async_copy(wmat_h, wmat, lsem.at[2])
    small = [(table_h.at[gy], table), (spread_h, spread), (dz_h, dz), (ys_h, ys), (wr_h, wr)]
    small = [pltpu.make_async_copy(src, dst, lsem.at[3 + n]) for n, (src, dst) in enumerate(small)]
    load_ref.start()

    barrier = pltpu.get_barrier_semaphore()
    partners = [at(0, 1), at(0, -1), at(1, 0), at(-1, 0)]
    partners += [at(bx, by) for bx, by in SOURCES if bx != 0 and by != 0]
    partners += [at(0, m) for m in range(2, NGY - 1)] + [at(m, 0) for m in range(2, NGX - 1)]
    for partner in partners:
        pl.semaphore_signal(barrier, inc=1, device_id=partner, device_id_type=MESH)
    for copy in (*small, load_own, load_w):
        copy.start()

    def flag(condition):
        return jnp.where(condition, 1.0, 0.0).astype(F32)

    xlo_ok, xhi_ok = flag(gx > 0), flag(gx < NGX - 1)
    ylo_ok, yhi_ok = flag(gy > 0), flag(gy < NGY - 1)

    load_ref.wait()
    yface[0] = jnp.concatenate([ref_v[x, 24:32, :].astype(F32)[7:8] for x in range(32)], axis=0).astype(BF16)
    yface[1] = jnp.concatenate([ref_v[x, 0:8, :].astype(F32)[0:1] for x in range(32)], axis=0).astype(BF16)

    pl.semaphore_wait(barrier, len(partners))

    def send(src, dst, s, r, to):
        pltpu.make_async_remote_copy(
            src_ref=src, dst_ref=dst, send_sem=s, recv_sem=r, device_id=to, device_id_type=MESH
        ).start()

    def wait(as_much, sem):
        pltpu.make_async_copy(as_much, as_much, sem).wait()

    send(yface.at[0], faces.at[0], sems.at[0, 0], sems.at[0, 1], at(0, 1))
    send(yface.at[1], faces.at[1], sems.at[0, 0], sems.at[0, 1], at(0, -1))
    send(ref_v.at[31], faces.at[2], sems.at[0, 0], sems.at[0, 1], at(1, 0))
    send(ref_v.at[0], faces.at[3], sems.at[0, 0], sems.at[0, 1], at(-1, 0))
    load_own.wait()
    for part in range(2):
        rows = pl.ds(16 * part, 16)
        for side, dy in ((0, 1), (1, -1)):
            send(own_v.at[rows], def_v.at[side, rows], sems.at[1, 0], sems.at[(1, 7)[part], 1], at(0, dy))
    for copy in small:
        copy.wait()
    row = (table[...] - gy).astype(F32)
    r16 = lax.broadcasted_iota(jnp.int32, (16, 64), 0)
    c64 = lax.broadcasted_iota(jnp.int32, (16, 64), 1)
    picked = jnp.where(c64 // 4 == r16, jnp.broadcast_to(row, (16, 64)), 0.0).astype(BF16)
    mask_s[...] = mm(picked, spread[...])

    for x in range(32):
        plane = ref_v[x]
        fs[x + 1, 8:40, :] = plane.astype(F32)
        gs[2, x] = mm(plane, dz[...])
    wait(faces, sems.at[0, 1])
    fs[0, 8:40, :] = faces[2].astype(F32) * xlo_ok
    fs[33, 8:40, :] = faces[3].astype(F32) * xhi_ok
    face_lo = faces[0].astype(F32) * ylo_ok
    face_hi = faces[1].astype(F32) * yhi_ok
    for x in range(32):
        fs[x + 1, 7:8, :] = face_lo[x : x + 1]
        fs[x + 1, 40:41, :] = face_hi[x : x + 1]

    for ey in range(2):
        r = 8 + 16 * ey
        y = slice(16 * ey, 16 * ey + 16)
        moments = []
        for ex in range(2):
            def step(t, carry, ex=ex, r=r, y=y):
                x = 16 * ex + t
                g = (
                    fs[x + 2, r : r + 16, :] - fs[x, r : r + 16, :],
                    fs[x + 1, r + 1 : r + 17, :] - fs[x + 1, r - 1 : r + 15, :],
                    gs[2, x, y, :],
                )
                gs[0, x, y, :] = g[0]
                gs[1, x, y, :] = g[1]
                out = []
                for p, (c, d) in enumerate(PAIRS):
                    s1, s2, s3 = carry[p]
                    s1 = s1 + g[c] * g[d]
                    s2 = s2 + s1
                    s3 = s3 + s2
                    out.append((s1, s2, s3))
                return tuple(out)

            zero = jnp.zeros((16, 128), F32)
            sums = lax.fori_loop(0, 16, step, tuple((zero,) * 3 for _ in PAIRS), unroll=4)
            weighted = []
            for s1, s2, s3 in sums:
                m00 = (2.0 * s3 - s2) * (1.0 / 256.0)
                first = s2 * (1.0 / 16.0)
                weighted.append((m00, first - m00, s1 - 2.0 * first + m00))
            moments.append(weighted)
        for p in range(6):
            (a00, a01, a11), (b00, b01, b11) = moments[0][p], moments[1][p]
            rows = slice(p * 32 + 16 * ey, p * 32 + 16 * ey + 16)
            for u, value in enumerate((a00, a01, a11 + b00, b01, b11)):
                xs[u, rows, :] = value

    ymat = ys[:48, :]
    t2[40:48, :] = jnp.zeros((8, 640), F32)
    for u in range(5):
        hi, mid, low = pieces(xs[u])
        t = mm(ymat, hi) + mm(ymat, mid) + mm(ymat, low)
        for m in range(5):
            t2[8 * u : 8 * u + 8, 128 * m : 128 * m + 128] = t[8 * m : 8 * m + 8]
    load_w.wait()
    stacked = jnp.concatenate(pieces(t2[...]), axis=0)
    done = mm(stacked, wmat[...])
    done = done[:48] + done[48:96] + done[96:144]
    for u in range(5):
        for group in range(4):
            ksend[group, u] = done[8 * u : 8 * u + 8, 128 * group : 128 * group + 128]

    GROUP = {1: (0, 1), 0: (1, 2), -1: (3, 1)}
    UNIT = {1: (1, 4), 0: (0, 5), -1: (0, 2)}
    for dx, dy in NEIGHBOURS:
        g0, gn = GROUP[dy]
        u0, un = UNIT[dx]
        send(
            ksend.at[pl.ds(g0, gn), pl.ds(u0, un)],
            krecv.at[1 - dx, pl.ds(g0, gn), pl.ds(u0, un)],
            sems.at[2, 0], sems.at[2, 1], at(dx, dy),
        )
    krecv[1, 1:3] = ksend[1:3]

    lane = lax.broadcasted_iota(jnp.int32, (8, 128), 1)
    sub = lax.broadcasted_iota(jnp.int32, (8, 128), 0)

    parts = {}
    for ex in range(2):
        wait(def_v.at[:, pl.ds(16 * ex, 16)], sems.at[(1, 7)[ex], 1])
        for ey in range(2):
            r = 8 + 16 * ey
            y = slice(16 * ey, 16 * ey + 16)
            carry = tuple((jnp.zeros((16, 128), F32),) * 2 for _ in range(3))
            for xb in range(2):
                k = (2 * ex + xb) * 4 + 2 * ey
                off = jnp.concatenate(
                    [jnp.broadcast_to(mask_s[k + h : k + h + 1, :], (8, 128)) for h in range(2)], axis=0
                )
                below, above = off < -0.5, off > 0.5

                def step(t, carry, below=below, above=above, ex=ex, xb=xb, r=r, y=y):
                    x = 16 * ex + 8 * xb + t
                    warped = jnp.where(
                        below, def_v[0, x, y, :].astype(F32),
                        jnp.where(above, def_v[1, x, y, :].astype(F32), own_v[x, y, :].astype(F32)),
                    )
                    misfit = fs[x + 1, r : r + 16, :] - warped
                    out = []
                    for c in range(3):
                        s1, s2 = carry[c]
                        s1 = s1 + gs[c, x, y, :] * misfit
                        out.append((s1, s2 + s1))
                    return tuple(out)

                carry = lax.fori_loop(0, 8, step, carry, unroll=4)
            parts[ex, ey] = [(s2 * (1.0 / 16.0), s1 - s2 * (1.0 / 16.0)) for s1, s2 in carry]
    for ey in range(2):
        for c in range(3):
            (a0, a1_), (b0, b1_) = parts[0, ey][c], parts[1, ey][c]
            rows = slice(c * 32 + 16 * ey, c * 32 + 16 * ey + 16)
            for n, value in enumerate((a0, a1_ + b0, b1_)):
                rx[n, rows, :] = value
    yr = ys[48:, :96]
    rt2[24:32, :] = jnp.zeros((8, 384), F32)
    for n in range(3):
        hi, mid, low = pieces(rx[n])
        t = mm(yr, hi) + mm(yr, mid) + mm(yr, low)
        for m in range(3):
            rt2[8 * n : 8 * n + 8, 128 * m : 128 * m + 128] = t[8 * m : 8 * m + 8]
    stacked = jnp.concatenate(pieces(rt2[...]), axis=0)
    done = mm(stacked, wr[...])
    done = done[:32] + done[32:64] + done[64:96]
    rsend[...] = jnp.where(lane < 64, jnp.where(sub < 3, done[:8], done[8:16]), done[16:24])
    for bx, by in SOURCES:
        send(rsend, rrecv.at[4 * bx + by + 10], sems.at[3, 0], sems.at[3, 1], at(-bx, -by))
    rrecv[10] = rsend[...]

    slot, depth = lane // 16, lane % 16

    def roll(x, shift):
        shift = shift % 128
        return x if shift == 0 else pltpu.roll(x, shift, 1)

    wait(ktotal, sems.at[2, 1])
    in_a_diag = jnp.where(slot == 1, 1.0, jnp.where(slot == 2, ylo_ok, 0.0))
    in_b_diag = (slot >= 2) & (slot <= 4)
    for e in range(9):
        def entry(group, e=e):
            if e == 3:
                return krecv[0, group, 4] * xlo_ok + krecv[1, group, 0]
            if e == 7:
                return krecv[1, group, 4] + krecv[2, group, 0]
            if e < 3:
                return krecv[0, group, e + 1]
            if e < 7:
                return krecv[1, group, e - 3]
            return krecv[2, group, 1]

        a, b0, b1_, c = [entry(group) for group in range(4)]

        def diag(a, b, c):
            return a * in_a_diag + jnp.where(in_b_diag, b, 0.0) + jnp.where(slot == 4, c, 0.0)

        def off_diag(a, b, c):
            return jnp.where(slot < 2, a, jnp.where(slot < 4, b, jnp.where(slot == 4, c, 0.0)))

        dd = diag(roll(a, -16), b0, c)
        fd = off_diag(a, roll(b0, -48), roll(c, -16))
        df = diag(roll(a, -80), b1_, roll(c, -32))
        ff = off_diag(roll(a, -64), roll(b1_, -48), roll(c, -48))
        kf[e, 4] = dd
        kf[e, 5] = df
        kf[e, 3] = roll(df, 1)
        kf[e, 7] = fd
        kf[e, 1] = roll(fd, 16)
        kf[e, 8] = ff
        kf[e, 6] = roll(ff, 1)
        kf[e, 2] = roll(ff, 16)
        kf[e, 0] = roll(ff, 17)

    lane_j = 2 * gy + slot - 2
    lane_ok = (lane_j >= 0) & (lane_j < 64) & (slot < 6) & (depth < 9)
    lane_mask = jnp.where(lane_ok, 1.0, 0.0)
    node_mask = {i: lane_mask * flag((2 * gx + i >= 0) & (2 * gx + i < 16)) for i in range(-2, 4)}
    own_mask = jnp.where((slot >= 2) & (slot < 4) & (depth < 9), 1.0, 0.0)

    def apply(v, rows):
        need = sorted({i + ox for i in rows for ox in (-1, 0, 1)})
        first, second = {}, {}
        for i in need:
            second[i] = v[i]
            first[i] = jnp.where(sub < 3, v[i], pltpu.roll(v[i], 7, 0))
        acc1 = {i: jnp.zeros((8, 128), F32) for i in rows}
        acc2 = {i: jnp.zeros((8, 128), F32) for i in rows}
        for o in range(9):
            oy, oz = o // 3 - 1, o % 3 - 1
            s1 = {i: roll(first[i], -(16 * oy + oz)) for i in need}
            s2 = {i: roll(second[i], -(16 * oy + oz)) for i in need}
            for i in rows:
                for ox in (-1, 0, 1):
                    k = kf[2 * i + 3 + ox, o]
                    acc1[i] = acc1[i] + k * s1[i + ox]
                    acc2[i] = acc2[i] + k * s2[i + ox]
        out = {}
        for i in rows:
            total = acc1[i] + pltpu.roll(acc1[i], 5, 0)
            total = total + jnp.where(sub == 0, pltpu.roll(acc2[i], 3, 0), pltpu.roll(acc2[i], 6, 0))
            out[i] = jnp.where(sub < 3, total, jnp.where(sub < 6, pltpu.roll(total, 3, 0), pltpu.roll(total, 6, 0)))
        return out

    wait(rrecv.at[pl.ds(0, 15)], sems.at[3, 1])
    w0 = {}
    lo2_x, lo2_y = flag(gx > 1), flag(gy > 1)
    x_ok = {-2: lo2_x, -1: xlo_ok, 0: None, 1: None}
    y_ok = {-2: lo2_y, -1: ylo_ok, 0: None, 1: None}
    totals = {i: None for i in range(-2, 4)}
    for by in (-2, -1, 0, 1):
        part = {i: None for i in range(-2, 4)}
        for bx in (-2, -1, 0, 1):
            tile = rrecv[4 * bx + by + 10]
            if x_ok[bx] is not None:
                tile = tile * x_ok[bx]
            for n in range(3):
                i = 2 * bx + n
                if i in part:
                    shifted = (tile, pltpu.roll(tile, 5, 0), roll(tile, 64))[n]
                    part[i] = add(part[i], shifted)
        for i in part:
            here = jnp.where(lane < 48, part[i], 0.0)
            if y_ok[by] is not None:
                here = here * y_ok[by]
            totals[i] = add(totals[i], roll(here, 32 * (by + 1)))
    for i in totals:
        t = totals[i]
        t = jnp.where(sub < 3, t, jnp.where(sub < 6, pltpu.roll(t, 3, 0), pltpu.roll(t, 6, 0)))
        w0[i] = t * node_mask[i]

    w1 = apply(w0, (-1, 0, 1, 2))
    w1 = {i: w1[i] * node_mask[i] for i in w1}
    w2_own = apply(w1, (0, 1))
    vsend[...] = jnp.where(sub < 3, w2_own[0], w2_own[1]) * own_mask
    for dx, dy in NEIGHBOURS:
        send(vsend, vrecv.at[4 - 3 * dx - dy], sems.at[4, 0], sems.at[4, 1], at(dx, dy))
    vrecv[4] = vsend[...]

    wait(vrecv.at[pl.ds(0, 8)], sems.at[4, 1])
    w2 = {}
    for i in range(-2, 4):
        if i % 2 == 0:
            b = 3 * (i // 2) + 4
            t = vrecv[b] + roll(vrecv[b - 1], -32) + roll(vrecv[b + 1], 32)
            back, ahead = pltpu.roll(t, 5, 0), pltpu.roll(t, 3, 0)
            total = jnp.where(sub < 3, t, jnp.where(sub < 6, ahead, pltpu.roll(t, 6, 0)))
        else:
            total = jnp.where(sub < 3, back, jnp.where(sub < 6, t, ahead))
        w2[i] = total * node_mask[i]
    w3 = apply(w2, (-1, 0, 1, 2))
    w3 = {i: w3[i] * node_mask[i] for i in w3}
    w4 = apply(w3, (0, 1))
    krylov = [w0, w1, w2, w3, w4]

    packed = [jnp.where(sub < 3, w[0], jnp.where(sub < 6, w[1], 0.0)) * own_mask for w in krylov]
    left = roll(packed[0], -32) + packed[1] + roll(packed[2], 32) + roll(packed[3], 64)
    left_halves = split(left)
    value = remainder = jnp.zeros((8, 128), F32)
    for j in range(5):
        right = packed[j] + roll(packed[j], 32)
        right = right + roll(right, 64)
        p, e = two_prod(left, left_halves, right, split(right))
        for shift in (4, 2, 1):
            p, err = two_sum(p, pltpu.roll(p, shift, 0))
            e = e + pltpu.roll(e, shift, 0) + err
        value = jnp.where(sub == j, p, value)
        remainder = jnp.where(sub == j, e, remainder)

    for shift in (16, 8, 4, 2, 1):
        remainder = remainder + roll(remainder, -shift)
        value, err = two_sum(value, roll(value, -shift))
        remainder = remainder + err
    line = jnp.zeros((1, 128), F32)
    first = (lane % 32 == 0)[:1]
    for j in range(5):
        line = line + roll(jnp.where(first, value[j : j + 1], 0.0), j)
        line = line + roll(jnp.where(first, remainder[j : j + 1], 0.0), 8 + j)

    def line_tree(slots):
        p, e = slots, None
        while p.shape[0] > 1:
            half = p.shape[0] // 2
            p, err = two_sum(p[:half], p[half:])
            e = err if e is None else e[:half] + e[half:] + err
        return p[0], e[0]

    asrc[...] = line
    a1[gy] = line
    for m in FAR_Y:
        send(asrc, a1.at[gy], sems.at[5, 0], sems.at[5, 1], at(0, m))
    wait(a1.at[pl.ds(0, NGY - 1)], sems.at[5, 1])
    p, e = line_tree(a1[...])
    line = jnp.where((lane % 16 < 8)[:1], p, p + roll(e, 8))
    b1src[...] = line
    b1[gx] = line
    for m in FAR_X:
        send(b1src, b1.at[gx], sems.at[6, 0], sems.at[6, 1], at(m, 0))
    wait(b1.at[pl.ds(0, NGX - 1)], sems.at[6, 1])
    p, e = line_tree(b1[...])
    e = e + roll(p, -8)
    high = p + e
    low = (p - high) + e

    def few_bits(x):
        t = x * 262145.0
        return t - (t - x)

    m0, m1, m2 = [jnp.broadcast_to(high[:, n : n + 1], (8, 128)) for n in (0, 1, 33)]
    mean = m1 / m0
    mu = few_bits(mean)
    spread_q = few_bits(jnp.maximum(m2 / m0 - mean * mean, 1e-5 * mean * mean))
    poly = [[jnp.ones_like(m0)]]
    for k in range(4):
        new = [None] + list(poly[k])
        for i, a in enumerate(poly[k]):
            new[i] = add(new[i], -(mu * a))
        if k:
            for i, a in enumerate(poly[k - 1]):
                new[i] = new[i] - spread_q * a
        poly.append(new)

    def combine(coefficients, terms):
        total = None
        for c, (h, l) in zip(coefficients, terms):
            c = c[: h.shape[0]]
            p, e = two_prod(c, split(c), h, split(h))
            e = e + c * l
            if total is None:
                total = (p, e)
            else:
                q, err = two_sum(total[0], p)
                total = (q, total[1] + e + err)
        h = total[0] + total[1]
        return h, (total[0] - h) + total[1]

    rows_w = [(roll(high, -j), roll(low, -j)) for j in range(5)]
    rows_q = [combine(poly[k], rows_w) for k in range(5)]
    filler = [jnp.zeros((3, 128), F32)]
    mixed = [jnp.concatenate([r[n] for r in rows_q] + filler, axis=0) for n in range(2)]
    moved = [tuple(roll(x, -32 * t) for x in mixed) for t in range(4)]
    G = {}
    for l in range(4):
        h, _ = combine(poly[l], moved)
        for k in range(l, 5):
            G[k, l] = G[l, k] = jnp.broadcast_to(h[k : k + 1, 0:1], (8, 128))

    own = (0, 1)

    def times(k_of, v, older):
        return {i: k_of[i] - mu * v[i] - (0.0 if older is None else spread_q * older[i]) for i in own}

    q1 = times(w1, w0, None)
    kq1 = times(w2, w1, None)
    kkq1 = times(w3, w2, None)
    kkkq1 = times(w4, w3, None)
    q2 = times(kq1, q1, w0)
    kq2 = times(kkq1, kq1, w1)
    kkq2 = times(kkkq1, kkq1, w2)
    q3 = times(kq2, q2, q1)
    kq3 = times(kkq2, kq2, kq1)
    q4 = times(kq3, q3, q2)
    basis = [w0, q1, q2, q3, q4]

    def form(left, right):
        total = None
        for i, a in enumerate(left):
            if a is None:
                continue
            inner = None
            for j, b in enumerate(right):
                if b is None:
                    continue
                term = G[i, j] * b
                inner = term if inner is None else inner + term
            term = a * inner
            total = term if total is None else total + term
        return total

    one = jnp.ones_like(m0)
    center = mu + DAMPING
    residual = [one, None, None, None, None]
    direction = list(residual)
    update = [None] * 5
    rr = G[0, 0]
    for turn in range(ITERS):
        image = [None] * 5
        for k in range(4):
            d = direction[k]
            if d is None:
                continue
            image[k] = add(image[k], center * d)
            image[k + 1] = add(image[k + 1], d)
            if k:
                image[k - 1] = add(image[k - 1], spread_q * d)
        alpha = rr / form(direction, image)
        update = [add(u, None if d is None else alpha * d) for u, d in zip(update, direction)]
        residual = [add(r, None if q is None else -(alpha * q)) for r, q in zip(residual, image)]
        if turn < ITERS - 1:
            new = form(residual, residual)
            beta = new / rr
            direction = [add(r, None if d is None else beta * d) for r, d in zip(residual, direction)]
            rr = new
    for first_row, coords in ((0, update), (3, residual)):
        for i in range(2):
            total = None
            for k in range(5):
                if coords[k] is not None:
                    term = coords[k] * basis[k][i]
                    total = term if total is None else total + term
            for j in range(2):
                moved = roll(total, -(32 + 16 * j))
                for c in range(3):
                    out_ref[first_row + c, i, j : j + 1, :] = moved[c : c + 1, :9]

    sent = (faces, def_v, ktotal, rrecv.at[pl.ds(0, 15)], vrecv.at[pl.ds(0, 8)], a1.at[pl.ds(0, NGY - 1)], b1.at[pl.ds(0, NGX - 1)])
    for n, as_much in enumerate(sent):
        wait(as_much, sems.at[n, 0])


def local(reference_scan, deformed_scan, source_column):
    table = source_column.reshape(NGY, 1, 64)
    consts = constants()
    vmem = pl.BlockSpec(memory_space=pltpu.VMEM)
    hbm = pl.BlockSpec(memory_space=pltpu.HBM)
    V, DMA = pltpu.VMEM, pltpu.SemaphoreType.DMA
    scratch = [
        V((1, 64), jnp.int32), V((80, 192), BF16), V((384, 128), BF16), V((128, 128), BF16), V((64, 128), BF16),
        V((32, 32, 128), BF16), V((32, 32, 128), BF16), V((2, 32, 32, 128), BF16),
        V((34, 48, 128), F32), V((3, 32, 32, 128), F32), V((16, 128), F32),
        V((2, 32, 128), BF16), V((4, 32, 128), BF16),
        V((5, 192, 128), F32), V((48, 640), F32), V((4, 5, 8, 128), F32), V((3, 4, 5, 8, 128), F32),
        V((3, 96, 128), F32), V((32, 384), F32), V((8, 128), F32), V((16, 8, 128), F32),
        V((9, 9, 8, 128), F32), V((640, 512), BF16), V((8, 128), F32), V((9, 8, 128), F32),
        V((1, 128), F32), V((NGY, 1, 128), F32), V((1, 128), F32), V((NGX, 1, 128), F32),
        V((34, 8, 128), F32), DMA((8,)), DMA((8, 2)),
    ]
    both = pl.pallas_call(
        kernel,
        out_shape=jax.ShapeDtypeStruct((6, 2, 2, 9), F32),
        in_specs=[hbm] * 8,
        out_specs=vmem,
        scratch_shapes=scratch,
        compiler_params=pltpu.CompilerParams(
            collective_id=0, has_side_effects=True, vmem_limit_bytes=55210 * 1024
        ),
    )(reference_scan, deformed_scan, table, *consts)
    return both[:3], both[3:]


def solution(mesh):
    return jax.shard_map(
        local,
        mesh=mesh,
        in_specs=(P("gx", "gy", None), P("gx", "gy", None), P("gx", None, None, None)),
        out_specs=(P(None, "gx", "gy", None), P(None, "gx", "gy", None)),
        check_vma=False,
    )
```

```python
import functools

import jax
import jax.numpy as jnp
import ml_dtypes
import numpy as np
from jax import lax
from jax.experimental import pallas as pl
from jax.experimental.pallas import tpu as pltpu
from jax.sharding import PartitionSpec as P

MESH = pl.DeviceIdType.MESH
E = 16
ITERS = 4
DAMPING = 0.1
KSCALE = 4.0
NGX, NGY = 8, 32
F32, BF16 = jnp.float32, jnp.bfloat16

NEIGHBOURS = [(dx, dy) for dx in (-1, 0, 1) for dy in (-1, 0, 1) if (dx, dy) != (0, 0)]
SOURCES = [(bx, by) for bx in (-2, -1, 0, 1) for by in (-2, -1, 0, 1) if (bx, by) != (0, 0)]
SOURCES.sort(key=lambda b: -abs(b[0]) - 0.9 * abs(b[1]))
NEIGHBOURS.sort(key=lambda b: -abs(b[0]) - abs(b[1]))
FAR_Y = sorted(range(1, NGY), key=lambda m: -min(m // 8, 4 - m // 8) - min(m % 8, 8 - m % 8) / 2)
FAR_X = sorted(range(1, NGX), key=lambda m: -min(m, NGX - m))
PAIRS = [(0, 0), (1, 1), (2, 2), (0, 1), (1, 2), (2, 0)]


def hat(position):
    return np.maximum(0.0, 1.0 - np.abs(position) / E)


def chain(count, nodes):
    position = np.arange(count)
    w = np.stack([hat(position - E * n) for n in range(nodes)])
    out = []
    for n in range(nodes):
        out.append(w[n] * w[n])
        if n + 1 < nodes:
            out.append(w[n] * w[n + 1])
    return w, np.stack(out)


def constants():
    wy, cy = chain(32, 3)
    wz, cz = chain(128, 9)
    scale = 1.0 / (1024.0 * KSCALE)
    ymat = np.zeros((48, 192))
    for m in range(5):
        for p in range(6):
            ymat[m * 8 + p, p * 32 : (p + 1) * 32] = cy[m] * scale
    zd, zf = np.zeros((128, 16)), np.zeros((128, 16))
    zd[:, :9] = cz[0::2].T
    zf[:, :8] = cz[1::2].T
    wmat = np.zeros((5, 128, 4, 8, 16))
    D0, F0, D1, F1, D2 = range(5)
    place = {
        (0, 0): (F0, zd), (0, 1): (F1, zd), (0, 2): (D1, zd), (0, 3): (D2, zd),
        (0, 4): (F0, zf), (0, 5): (F1, zf), (0, 6): (D1, zf), (0, 7): (D2, zf),
        (1, 2): (D0, zd), (1, 3): (D1, zd), (1, 4): (D2, zd), (1, 5): (F0, zd), (1, 6): (F1, zd),
        (2, 2): (D0, zf), (2, 3): (D1, zf), (2, 4): (D2, zf), (2, 5): (F0, zf), (2, 6): (F1, zf),
        (3, 4): (D0, zd), (3, 5): (F0, zd), (3, 6): (D0, zf), (3, 7): (F0, zf),
    }
    for (group, block), (m, z) in place.items():
        wmat[m, :, group, block, :] = z
    wmat = wmat.reshape(640, 512)
    yr = np.zeros((32, 96))
    for n in range(3):
        for r in range(8):
            c = r % 3
            yr[n * 8 + r, c * 32 : (c + 1) * 32] = wy[n] / 32.0
    wr = np.zeros((3, 128, 8, 16))
    for n in range(3):
        wr[n, :, n, :9] = wr[n, :, 4 + n, :9] = wz.T
    wr = wr.reshape(384, 128)
    dz = np.zeros((128, 128))
    for z in range(128):
        if z + 1 < 128:
            dz[z + 1, z] = 1.0
        if z > 0:
            dz[z - 1, z] = -1.0
    lanes = np.arange(128)
    spread = (np.arange(64)[:, None] % 4 == lanes[None, :] // 32).astype(np.float64)
    cast = lambda a: a.astype(ml_dtypes.bfloat16)
    both = np.zeros((80, 192))
    both[:48] = ymat
    both[48:, :96] = yr
    return [cast(a) for a in (both, wmat, wr, dz, spread)]


def pieces(x):
    hi = x.astype(BF16)
    rest = x - hi.astype(F32)
    mid = rest.astype(BF16)
    low = (rest - mid.astype(F32)).astype(BF16)
    return hi, mid, low


def two_sum(a, b):
    s = a + b
    t = s - a
    return s, (a - (s - t)) + (b - t)


def split(a):
    t = a * 4097.0
    high = t - (t - a)
    return high, a - high


def two_prod(a, a_halves, b, b_halves):
    p = a * b
    (ah, al), (bh, bl) = a_halves, b_halves
    return p, ((ah * bh - p) + ah * bl + al * bh) + al * bl


def add(a, b):
    return b if a is None else (a if b is None else a + b)


def mm(a, b):
    return jnp.dot(a, b, preferred_element_type=F32)


def kernel(
    ref_h, def_h, table_h, ys_h, wmat_h, wr_h, dz_h, spread_h,
    out_ref,
    table, ys, wr, dz, spread,
    ref_v, own_v, def_v, fs, gs, mask_s, yface, faces,
    xs, t2, ksend, krecv, rx, rt2, rsend, rrecv, kf, wmat, vsend, vrecv,
    asrc, a1, b1src, b1,
    ktotal, lsem, sems,
):
    gx, gy = lax.axis_index("gx"), lax.axis_index("gy")

    gx_at = [lax.rem(gx + d, NGX) for d in range(NGX)]
    gy_at = [lax.rem(gy + d, NGY) for d in range(NGY)]

    def at(dx, dy):
        return (gx_at[dx % NGX], gy_at[dy % NGY])

    load_ref = pltpu.make_async_copy(ref_h, ref_v, lsem.at[0])
    load_own = pltpu.make_async_copy(def_h, own_v, lsem.at[1])
    load_w = pltpu.make_async_copy(wmat_h, wmat, lsem.at[2])
    small = [(table_h.at[gy], table), (spread_h, spread), (dz_h, dz), (ys_h, ys), (wr_h, wr)]
    small = [pltpu.make_async_copy(src, dst, lsem.at[3 + n]) for n, (src, dst) in enumerate(small)]
    load_ref.start()

    barrier = pltpu.get_barrier_semaphore()
    partners = [at(0, 1), at(0, -1), at(1, 0), at(-1, 0)]
    partners += [at(bx, by) for bx, by in SOURCES if bx != 0 and by != 0]
    partners += [at(0, m) for m in range(2, NGY - 1)] + [at(m, 0) for m in range(2, NGX - 1)]
    for partner in partners:
        pl.semaphore_signal(barrier, inc=1, device_id=partner, device_id_type=MESH)
    for copy in (*small, load_own, load_w):
        copy.start()

    def flag(condition):
        return jnp.where(condition, 1.0, 0.0).astype(F32)

    xlo_ok, xhi_ok = flag(gx > 0), flag(gx < NGX - 1)
    ylo_ok, yhi_ok = flag(gy > 0), flag(gy < NGY - 1)

    load_ref.wait()
    yface[0] = jnp.concatenate([ref_v[x, 24:32, :].astype(F32)[7:8] for x in range(32)], axis=0).astype(BF16)
    yface[1] = jnp.concatenate([ref_v[x, 0:8, :].astype(F32)[0:1] for x in range(32)], axis=0).astype(BF16)

    pl.semaphore_wait(barrier, len(partners))

    def send(src, dst, s, r, to):
        pltpu.make_async_remote_copy(
            src_ref=src, dst_ref=dst, send_sem=s, recv_sem=r, device_id=to, device_id_type=MESH
        ).start()

    def wait(as_much, sem):
        pltpu.make_async_copy(as_much, as_much, sem).wait()

    send(yface.at[0], faces.at[0], sems.at[0, 0], sems.at[0, 1], at(0, 1))
    send(yface.at[1], faces.at[1], sems.at[0, 0], sems.at[0, 1], at(0, -1))
    send(ref_v.at[31], faces.at[2], sems.at[0, 0], sems.at[0, 1], at(1, 0))
    send(ref_v.at[0], faces.at[3], sems.at[0, 0], sems.at[0, 1], at(-1, 0))
    load_own.wait()
    for part in range(2):
        rows = pl.ds(16 * part, 16)
        for side, dy in ((0, 1), (1, -1)):
            send(own_v.at[rows], def_v.at[side, rows], sems.at[1, 0], sems.at[(1, 7)[part], 1], at(0, dy))
    for copy in small:
        copy.wait()
    row = (table[...] - gy).astype(F32)
    r16 = lax.broadcasted_iota(jnp.int32, (16, 64), 0)
    c64 = lax.broadcasted_iota(jnp.int32, (16, 64), 1)
    picked = jnp.where(c64 // 4 == r16, jnp.broadcast_to(row, (16, 64)), 0.0).astype(BF16)
    mask_s[...] = mm(picked, spread[...])

    for x in range(32):
        plane = ref_v[x]
        fs[x + 1, 8:40, :] = plane.astype(F32)
        gs[2, x] = mm(plane, dz[...])
    wait(faces, sems.at[0, 1])
    fs[0, 8:40, :] = faces[2].astype(F32) * xlo_ok
    fs[33, 8:40, :] = faces[3].astype(F32) * xhi_ok
    face_lo = faces[0].astype(F32) * ylo_ok
    face_hi = faces[1].astype(F32) * yhi_ok
    for x in range(32):
        fs[x + 1, 7:8, :] = face_lo[x : x + 1]
        fs[x + 1, 40:41, :] = face_hi[x : x + 1]

    for ey in range(2):
        r = 8 + 16 * ey
        y = slice(16 * ey, 16 * ey + 16)
        moments = []
        for ex in range(2):
            def step(t, carry, ex=ex, r=r, y=y):
                x = 16 * ex + t
                g = (
                    fs[x + 2, r : r + 16, :] - fs[x, r : r + 16, :],
                    fs[x + 1, r + 1 : r + 17, :] - fs[x + 1, r - 1 : r + 15, :],
                    gs[2, x, y, :],
                )
                gs[0, x, y, :] = g[0]
                gs[1, x, y, :] = g[1]
                out = []
                for p, (c, d) in enumerate(PAIRS):
                    s1, s2, s3 = carry[p]
                    s1 = s1 + g[c] * g[d]
                    s2 = s2 + s1
                    s3 = s3 + s2
                    out.append((s1, s2, s3))
                return tuple(out)

            zero = jnp.zeros((16, 128), F32)
            sums = lax.fori_loop(0, 16, step, tuple((zero,) * 3 for _ in PAIRS), unroll=4)
            weighted = []
            for s1, s2, s3 in sums:
                m00 = (2.0 * s3 - s2) * (1.0 / 256.0)
                first = s2 * (1.0 / 16.0)
                weighted.append((m00, first - m00, s1 - 2.0 * first + m00))
            moments.append(weighted)
        for p in range(6):
            (a00, a01, a11), (b00, b01, b11) = moments[0][p], moments[1][p]
            rows = slice(p * 32 + 16 * ey, p * 32 + 16 * ey + 16)
            for u, value in enumerate((a00, a01, a11 + b00, b01, b11)):
                xs[u, rows, :] = value

    ymat = ys[:48, :]
    t2[40:48, :] = jnp.zeros((8, 640), F32)
    for u in range(5):
        hi, mid, low = pieces(xs[u])
        t = mm(ymat, hi) + mm(ymat, mid) + mm(ymat, low)
        for m in range(5):
            t2[8 * u : 8 * u + 8, 128 * m : 128 * m + 128] = t[8 * m : 8 * m + 8]
    load_w.wait()
    stacked = jnp.concatenate(pieces(t2[...]), axis=0)
    done = mm(stacked, wmat[...])
    done = done[:48] + done[48:96] + done[96:144]
    for u in range(5):
        for group in range(4):
            ksend[group, u] = done[8 * u : 8 * u + 8, 128 * group : 128 * group + 128]

    GROUP = {1: (0, 1), 0: (1, 2), -1: (3, 1)}
    UNIT = {1: (1, 4), 0: (0, 5), -1: (0, 2)}
    for dx, dy in NEIGHBOURS:
        g0, gn = GROUP[dy]
        u0, un = UNIT[dx]
        send(
            ksend.at[pl.ds(g0, gn), pl.ds(u0, un)],
            krecv.at[1 - dx, pl.ds(g0, gn), pl.ds(u0, un)],
            sems.at[2, 0], sems.at[2, 1], at(dx, dy),
        )
    krecv[1, 1:3] = ksend[1:3]

    lane = lax.broadcasted_iota(jnp.int32, (8, 128), 1)
    sub = lax.broadcasted_iota(jnp.int32, (8, 128), 0)

    parts = {}
    for ex in range(2):
        wait(def_v.at[:, pl.ds(16 * ex, 16)], sems.at[(1, 7)[ex], 1])
        for ey in range(2):
            r = 8 + 16 * ey
            y = slice(16 * ey, 16 * ey + 16)
            carry = tuple((jnp.zeros((16, 128), F32),) * 2 for _ in range(3))
            for xb in range(2):
                k = (2 * ex + xb) * 4 + 2 * ey
                off = jnp.concatenate(
                    [jnp.broadcast_to(mask_s[k + h : k + h + 1, :], (8, 128)) for h in range(2)], axis=0
                )
                below, above = off < -0.5, off > 0.5

                def step(t, carry, below=below, above=above, ex=ex, xb=xb, r=r, y=y):
                    x = 16 * ex + 8 * xb + t
                    warped = jnp.where(
                        below, def_v[0, x, y, :].astype(F32),
                        jnp.where(above, def_v[1, x, y, :].astype(F32), own_v[x, y, :].astype(F32)),
                    )
                    misfit = fs[x + 1, r : r + 16, :] - warped
                    out = []
                    for c in range(3):
                        s1, s2 = carry[c]
                        s1 = s1 + gs[c, x, y, :] * misfit
                        out.append((s1, s2 + s1))
                    return tuple(out)

                carry = lax.fori_loop(0, 8, step, carry, unroll=4)
            parts[ex, ey] = [(s2 * (1.0 / 16.0), s1 - s2 * (1.0 / 16.0)) for s1, s2 in carry]
    for ey in range(2):
        for c in range(3):
            (a0, a1_), (b0, b1_) = parts[0, ey][c], parts[1, ey][c]
            rows = slice(c * 32 + 16 * ey, c * 32 + 16 * ey + 16)
            for n, value in enumerate((a0, a1_ + b0, b1_)):
                rx[n, rows, :] = value
    yr = ys[48:, :96]
    rt2[24:32, :] = jnp.zeros((8, 384), F32)
    for n in range(3):
        hi, mid, low = pieces(rx[n])
        t = mm(yr, hi) + mm(yr, mid) + mm(yr, low)
        for m in range(3):
            rt2[8 * n : 8 * n + 8, 128 * m : 128 * m + 128] = t[8 * m : 8 * m + 8]
    stacked = jnp.concatenate(pieces(rt2[...]), axis=0)
    done = mm(stacked, wr[...])
    done = done[:32] + done[32:64] + done[64:96]
    rsend[...] = jnp.where(lane < 64, jnp.where(sub < 3, done[:8], done[8:16]), done[16:24])
    for bx, by in SOURCES:
        send(rsend, rrecv.at[4 * bx + by + 10], sems.at[3, 0], sems.at[3, 1], at(-bx, -by))
    rrecv[10] = rsend[...]

    slot, depth = lane // 16, lane % 16

    def roll(x, shift):
        shift = shift % 128
        return x if shift == 0 else pltpu.roll(x, shift, 1)

    wait(ktotal, sems.at[2, 1])
    in_a_diag = jnp.where(slot == 1, 1.0, jnp.where(slot == 2, ylo_ok, 0.0))
    in_b_diag = (slot >= 2) & (slot <= 4)
    for e in range(9):
        def entry(group, e=e):
            if e == 3:
                return krecv[0, group, 4] * xlo_ok + krecv[1, group, 0]
            if e == 7:
                return krecv[1, group, 4] + krecv[2, group, 0]
            if e < 3:
                return krecv[0, group, e + 1]
            if e < 7:
                return krecv[1, group, e - 3]
            return krecv[2, group, 1]

        a, b0, b1_, c = [entry(group) for group in range(4)]

        def diag(a, b, c):
            return a * in_a_diag + jnp.where(in_b_diag, b, 0.0) + jnp.where(slot == 4, c, 0.0)

        def off_diag(a, b, c):
            return jnp.where(slot < 2, a, jnp.where(slot < 4, b, jnp.where(slot == 4, c, 0.0)))

        dd = diag(roll(a, -16), b0, c)
        fd = off_diag(a, roll(b0, -48), roll(c, -16))
        df = diag(roll(a, -80), b1_, roll(c, -32))
        ff = off_diag(roll(a, -64), roll(b1_, -48), roll(c, -48))
        kf[e, 4] = dd
        kf[e, 5] = df
        kf[e, 3] = roll(df, 1)
        kf[e, 7] = fd
        kf[e, 1] = roll(fd, 16)
        kf[e, 8] = ff
        kf[e, 6] = roll(ff, 1)
        kf[e, 2] = roll(ff, 16)
        kf[e, 0] = roll(ff, 17)

    lane_j = 2 * gy + slot - 2
    lane_ok = (lane_j >= 0) & (lane_j < 64) & (slot < 6) & (depth < 9)
    lane_mask = jnp.where(lane_ok, 1.0, 0.0)
    node_mask = {i: lane_mask * flag((2 * gx + i >= 0) & (2 * gx + i < 16)) for i in range(-2, 4)}
    own_mask = jnp.where((slot >= 2) & (slot < 4) & (depth < 9), 1.0, 0.0)

    def apply(v, rows):
        need = sorted({i + ox for i in rows for ox in (-1, 0, 1)})
        first, second = {}, {}
        for i in need:
            second[i] = v[i]
            first[i] = jnp.where(sub < 3, v[i], pltpu.roll(v[i], 7, 0))
        acc1 = {i: jnp.zeros((8, 128), F32) for i in rows}
        acc2 = {i: jnp.zeros((8, 128), F32) for i in rows}
        for o in range(9):
            oy, oz = o // 3 - 1, o % 3 - 1
            s1 = {i: roll(first[i], -(16 * oy + oz)) for i in need}
            s2 = {i: roll(second[i], -(16 * oy + oz)) for i in need}
            for i in rows:
                for ox in (-1, 0, 1):
                    k = kf[2 * i + 3 + ox, o]
                    acc1[i] = acc1[i] + k * s1[i + ox]
                    acc2[i] = acc2[i] + k * s2[i + ox]
        out = {}
        for i in rows:
            total = acc1[i] + pltpu.roll(acc1[i], 5, 0)
            total = total + jnp.where(sub == 0, pltpu.roll(acc2[i], 3, 0), pltpu.roll(acc2[i], 6, 0))
            out[i] = jnp.where(sub < 3, total, jnp.where(sub < 6, pltpu.roll(total, 3, 0), pltpu.roll(total, 6, 0)))
        return out

    wait(rrecv.at[pl.ds(0, 15)], sems.at[3, 1])
    w0 = {}
    lo2_x, lo2_y = flag(gx > 1), flag(gy > 1)
    x_ok = {-2: lo2_x, -1: xlo_ok, 0: None, 1: None}
    y_ok = {-2: lo2_y, -1: ylo_ok, 0: None, 1: None}
    totals = {i: None for i in range(-2, 4)}
    for by in (-2, -1, 0, 1):
        part = {i: None for i in range(-2, 4)}
        for bx in (-2, -1, 0, 1):
            tile = rrecv[4 * bx + by + 10]
            if x_ok[bx] is not None:
                tile = tile * x_ok[bx]
            for n in range(3):
                i = 2 * bx + n
                if i in part:
                    shifted = (tile, pltpu.roll(tile, 5, 0), roll(tile, 64))[n]
                    part[i] = add(part[i], shifted)
        for i in part:
            here = jnp.where(lane < 48, part[i], 0.0)
            if y_ok[by] is not None:
                here = here * y_ok[by]
            totals[i] = add(totals[i], roll(here, 32 * (by + 1)))
    for i in totals:
        t = totals[i]
        t = jnp.where(sub < 3, t, jnp.where(sub < 6, pltpu.roll(t, 3, 0), pltpu.roll(t, 6, 0)))
        w0[i] = t * node_mask[i]

    w1 = apply(w0, (-1, 0, 1, 2))
    w1 = {i: w1[i] * node_mask[i] for i in w1}
    w2_own = apply(w1, (0, 1))
    vsend[...] = jnp.where(sub < 3, w2_own[0], w2_own[1]) * own_mask
    for dx, dy in NEIGHBOURS:
        send(vsend, vrecv.at[4 - 3 * dx - dy], sems.at[4, 0], sems.at[4, 1], at(dx, dy))
    vrecv[4] = vsend[...]

    wait(vrecv.at[pl.ds(0, 8)], sems.at[4, 1])
    w2 = {}
    for i in range(-2, 4):
        if i % 2 == 0:
            b = 3 * (i // 2) + 4
            t = vrecv[b] + roll(vrecv[b - 1], -32) + roll(vrecv[b + 1], 32)
            back, ahead = pltpu.roll(t, 5, 0), pltpu.roll(t, 3, 0)
            total = jnp.where(sub < 3, t, jnp.where(sub < 6, ahead, pltpu.roll(t, 6, 0)))
        else:
            total = jnp.where(sub < 3, back, jnp.where(sub < 6, t, ahead))
        w2[i] = total * node_mask[i]
    w3 = apply(w2, (-1, 0, 1, 2))
    w3 = {i: w3[i] * node_mask[i] for i in w3}
    w4 = apply(w3, (0, 1))
    krylov = [w0, w1, w2, w3, w4]

    packed = [jnp.where(sub < 3, w[0], jnp.where(sub < 6, w[1], 0.0)) * own_mask for w in krylov]
    left = roll(packed[0], -32) + packed[1] + roll(packed[2], 32) + roll(packed[3], 64)
    left_halves = split(left)
    value = remainder = jnp.zeros((8, 128), F32)
    for j in range(5):
        right = packed[j] + roll(packed[j], 32)
        right = right + roll(right, 64)
        p, e = two_prod(left, left_halves, right, split(right))
        for shift in (4, 2, 1):
            p, err = two_sum(p, pltpu.roll(p, shift, 0))
            e = e + pltpu.roll(e, shift, 0) + err
        value = jnp.where(sub == j, p, value)
        remainder = jnp.where(sub == j, e, remainder)

    for shift in (16, 8, 4, 2, 1):
        remainder = remainder + roll(remainder, -shift)
        value, err = two_sum(value, roll(value, -shift))
        remainder = remainder + err
    line = jnp.zeros((1, 128), F32)
    first = (lane % 32 == 0)[:1]
    for j in range(5):
        line = line + roll(jnp.where(first, value[j : j + 1], 0.0), j)
        line = line + roll(jnp.where(first, remainder[j : j + 1], 0.0), 8 + j)

    def line_tree(slots):
        p, e = slots, None
        while p.shape[0] > 1:
            half = p.shape[0] // 2
            p, err = two_sum(p[:half], p[half:])
            e = err if e is None else e[:half] + e[half:] + err
        return p[0], e[0]

    asrc[...] = line
    a1[gy] = line
    for m in FAR_Y:
        send(asrc, a1.at[gy], sems.at[5, 0], sems.at[5, 1], at(0, m))
    wait(a1.at[pl.ds(0, NGY - 1)], sems.at[5, 1])
    p, e = line_tree(a1[...])
    line = jnp.where((lane % 16 < 8)[:1], p, p + roll(e, 8))
    b1src[...] = line
    b1[gx] = line
    for m in FAR_X:
        send(b1src, b1.at[gx], sems.at[6, 0], sems.at[6, 1], at(m, 0))
    wait(b1.at[pl.ds(0, NGX - 1)], sems.at[6, 1])
    p, e = line_tree(b1[...])
    e = e + roll(p, -8)
    high = p + e
    low = (p - high) + e

    def few_bits(x):
        t = x * 262145.0
        return t - (t - x)

    m0, m1, m2 = [jnp.broadcast_to(high[:, n : n + 1], (8, 128)) for n in (0, 1, 33)]
    mean = m1 / m0
    mu = few_bits(mean)
    spread_q = few_bits(jnp.maximum(m2 / m0 - mean * mean, 1e-5 * mean * mean))
    poly = [[jnp.ones_like(m0)]]
    for k in range(4):
        new = [None] + list(poly[k])
        for i, a in enumerate(poly[k]):
            new[i] = add(new[i], -(mu * a))
        if k:
            for i, a in enumerate(poly[k - 1]):
                new[i] = new[i] - spread_q * a
        poly.append(new)

    def combine(coefficients, terms):
        total = None
        for c, (h, l) in zip(coefficients, terms):
            c = c[: h.shape[0]]
            p, e = two_prod(c, split(c), h, split(h))
            e = e + c * l
            if total is None:
                total = (p, e)
            else:
                q, err = two_sum(total[0], p)
                total = (q, total[1] + e + err)
        h = total[0] + total[1]
        return h, (total[0] - h) + total[1]

    rows_w = [(roll(high, -j), roll(low, -j)) for j in range(5)]
    rows_q = [combine(poly[k], rows_w) for k in range(5)]
    filler = [jnp.zeros((3, 128), F32)]
    mixed = [jnp.concatenate([r[n] for r in rows_q] + filler, axis=0) for n in range(2)]
    moved = [tuple(roll(x, -32 * t) for x in mixed) for t in range(4)]
    G = {}
    for l in range(4):
        h, _ = combine(poly[l], moved)
        for k in range(l, 5):
            G[k, l] = G[l, k] = jnp.broadcast_to(h[k : k + 1, 0:1], (8, 128))

    own = (0, 1)

    def times(k_of, v, older):
        return {i: k_of[i] - mu * v[i] - (0.0 if older is None else spread_q * older[i]) for i in own}

    q1 = times(w1, w0, None)
    kq1 = times(w2, w1, None)
    kkq1 = times(w3, w2, None)
    kkkq1 = times(w4, w3, None)
    q2 = times(kq1, q1, w0)
    kq2 = times(kkq1, kq1, w1)
    kkq2 = times(kkkq1, kkq1, w2)
    q3 = times(kq2, q2, q1)
    kq3 = times(kkq2, kq2, kq1)
    q4 = times(kq3, q3, q2)
    basis = [w0, q1, q2, q3, q4]

    def form(left, right):
        total = None
        for i, a in enumerate(left):
            if a is None:
                continue
            inner = None
            for j, b in enumerate(right):
                if b is None:
                    continue
                term = G[i, j] * b
                inner = term if inner is None else inner + term
            term = a * inner
            total = term if total is None else total + term
        return total

    one = jnp.ones_like(m0)
    center = KSCALE * mu + DAMPING
    beside = KSCALE * spread_q
    residual = [one, None, None, None, None]
    direction = list(residual)
    update = [None] * 5
    rr = G[0, 0]
    for turn in range(ITERS):
        image = [None] * 5
        for k in range(4):
            d = direction[k]
            if d is None:
                continue
            image[k] = add(image[k], center * d)
            image[k + 1] = add(image[k + 1], KSCALE * d)
            if k:
                image[k - 1] = add(image[k - 1], beside * d)
        alpha = rr / form(direction, image)
        update = [add(u, None if d is None else alpha * d) for u, d in zip(update, direction)]
        residual = [add(r, None if q is None else -(alpha * q)) for r, q in zip(residual, image)]
        if turn < ITERS - 1:
            new = form(residual, residual)
            beta = new / rr
            direction = [add(r, None if d is None else beta * d) for r, d in zip(residual, direction)]
            rr = new
    for first_row, coords in ((0, update), (3, residual)):
        for i in range(2):
            total = None
            for k in range(5):
                if coords[k] is not None:
                    term = coords[k] * basis[k][i]
                    total = term if total is None else total + term
            for j in range(2):
                moved = roll(total, -(32 + 16 * j))
                for c in range(3):
                    out_ref[first_row + c, i, j : j + 1, :] = moved[c : c + 1, :9]

    sent = (faces, def_v, ktotal, rrecv.at[pl.ds(0, 15)], vrecv.at[pl.ds(0, 8)], a1.at[pl.ds(0, NGY - 1)], b1.at[pl.ds(0, NGX - 1)])
    for n, as_much in enumerate(sent):
        wait(as_much, sems.at[n, 0])


def local(reference_scan, deformed_scan, source_column):
    table = source_column.reshape(NGY, 1, 64)
    consts = constants()
    vmem = pl.BlockSpec(memory_space=pltpu.VMEM)
    hbm = pl.BlockSpec(memory_space=pltpu.HBM)
    V, DMA = pltpu.VMEM, pltpu.SemaphoreType.DMA
    scratch = [
        V((1, 64), jnp.int32), V((80, 192), BF16), V((384, 128), BF16), V((128, 128), BF16), V((64, 128), BF16),
        V((32, 32, 128), BF16), V((32, 32, 128), BF16), V((2, 32, 32, 128), BF16),
        V((34, 48, 128), F32), V((3, 32, 32, 128), F32), V((16, 128), F32),
        V((2, 32, 128), BF16), V((4, 32, 128), BF16),
        V((5, 192, 128), F32), V((48, 640), F32), V((4, 5, 8, 128), F32), V((3, 4, 5, 8, 128), F32),
        V((3, 96, 128), F32), V((32, 384), F32), V((8, 128), F32), V((16, 8, 128), F32),
        V((9, 9, 8, 128), F32), V((640, 512), BF16), V((8, 128), F32), V((9, 8, 128), F32),
        V((1, 128), F32), V((NGY, 1, 128), F32), V((1, 128), F32), V((NGX, 1, 128), F32),
        V((34, 8, 128), F32), DMA((8,)), DMA((8, 2)),
    ]
    both = pl.pallas_call(
        kernel,
        out_shape=jax.ShapeDtypeStruct((6, 2, 2, 9), F32),
        in_specs=[hbm] * 8,
        out_specs=vmem,
        scratch_shapes=scratch,
        compiler_params=pltpu.CompilerParams(
            collective_id=0, has_side_effects=True, vmem_limit_bytes=55210 * 1024
        ),
    )(reference_scan, deformed_scan, table, *consts)
    return both[:3], both[3:]


def solution(mesh):
    return jax.shard_map(
        local,
        mesh=mesh,
        in_specs=(P("gx", "gy", None), P("gx", "gy", None), P("gx", None, None, None)),
        out_specs=(P(None, "gx", "gy", None), P(None, "gx", "gy", None)),
        check_vma=False,
    )
```
